128 devices in a mesh: tile: 64 (over x, y, z_lo, core), sub: 2 (over z_hi).
Axes of the slice: x: 4, y: 4, z: 4 (z_hi: 2, z_lo: 2; z = z_hi * 2 + z_lo), core: 2. Of those that a mesh axis runs over, the one named last changes fastest.
Arguments:
- adjoint_flux: bfloat16 [6, 7, 2097152], P(None, None, ('tile', 'sub')), may hold values from -6 to 6
- ocean_wet: int32 [2097152], P(('tile', 'sub')), may hold values 0 or 1
- intersection_weight: bfloat16 [16384, 2, 128, 128], P(('tile', 'sub')), may hold values from -0.5 to 0.5
- pair_owner: int32 [16384, 2], P(('tile', 'sub')), may hold values from 0 to 127, all different within a row; in each aligned block of 128 rows (0 to 127, 128 to 255, ...) at most 4 rows name the same one
- pair_block: int32 [16384, 2], P(('tile', 'sub')), may hold values from 0 to 179
- land_sea: int32 [2048, 1440], P('tile', 'sub'), may hold values 0 or 1
- east_coef: float32 [2048, 1440], P('tile', 'sub'), may hold values from 0.03 to 0.24
- north_coef: float32 [2048, 1440], P('tile', 'sub'), may hold values from 0.03 to 0.24
Outputs:
- smoothed: float32 [14, 2048, 1440], P(None, 'tile', 'sub')
The draws below stay inside these ranges and needn't reach their ends.
Inputs may be any that keep to these rules, and one draw needn't show every extreme that they name: `pair_owner`: for each ocean block its 2 entries name different owners; among the rows of one device's 128 ocean blocks no owner is named more than 4 times, a bound that some block reaches. `pair_block`: control blocks of an owner are 8 rows by 16 longitudes, numbered along longitude first.
All inputs are finite; a program needn't handle non-finite values. No bound on the sum of `ocean_wet` or of `land_sea` on one device may be relied on, other than what follows from the above.
Results may differ from the reference program's by a relative error of at most 0.0029.
Values sent between devices are 32-bit elements; how exact they have to be, the bound alone decides.
A program may use at most 128 MiB of HBM per device.

```python
import math
import jax
import jax.numpy as jnp
import numpy as np
from jax import lax

FIELDS = 7
HOURS = 6
BLK = 128
TOP = 2
PASSES = 4
NLON = 1440
OB = 128
LAT_DEV = 32
CH = 14
LBW = 16
LON_DEV = 720
CB_DEV = 180
NLAT = 2048
NPAIRS = 16384
OCELLS = 2097152
CAP = 4
N_TILE = 64
N_SUB = 2
DEVICES = 128


def set_ends(array, rng, low, top_value):
    longest = array.shape.index(max(array.shape))
    spots = []
    for shift in (0, 1):
        where = [jax.random.randint(jax.random.fold_in(rng, axis), (), 0, length) for axis, length in enumerate(array.shape)]
        where[longest] = (where[longest] + shift) % array.shape[longest]
        spots.append(tuple(where))
    return array.at[spots[0]].set(low).at[spots[1]].set(top_value)


def steps_of(own_key, dims, cuts, low, largest):
    def one(dim, parts):
        draws = jax.random.uniform(jax.random.fold_in(jax.random.fold_in(own_key, 6), dim), (parts,), jnp.float32, low / len(cuts), largest / len(cuts))
        return jnp.repeat(jnp.exp(draws), dims[dim] // parts).reshape((-1,) + (1,) * (len(dims) - dim - 1))

    loudness = one(*cuts[0])
    for cut in cuts[1:]:
        loudness = loudness * one(*cut)
    return loudness


def assign_block(own_key, own, number, rows, amount, top, most, slope):
    order = jax.random.permutation(own_key, amount)
    heavy_load, usual = load_shares(amount, rows * top, most, slope, True), load_shares(amount, rows * top, most, slope, False)
    places = jnp.arange(amount)

    def named(lengths, offset_by):
        used = int((lengths > 0).sum())
        fixed = max(1, used // 4)
        shifted = fixed + (places - fixed + offset_by * (used - fixed)) % max(1, amount - fixed)
        return jnp.zeros((amount,), jnp.int32).at[order[jnp.where(places < fixed, places, shifted)]].set(jnp.asarray(lengths, jnp.int32))

    lengths = jnp.where(number % 4 == 0, named(heavy_load, number // 4), named(usual, number - number // 4 - 1))
    mixed = jax.random.permutation(jax.random.fold_in(own, 3), amount)
    giver, sink = mixed[0:amount // 2 * 2:2], mixed[1:amount // 2 * 2:2]
    slack = jnp.minimum(lengths[giver] - 1, most - lengths[sink]) // 2
    slack = jnp.where((giver == order[0]) | (sink == order[0]) | (lengths[sink] == 0), 0, jnp.maximum(slack, 0))
    shifted = jax.random.randint(jax.random.fold_in(own, 4), (amount // 2,), 0, 1 << 20) % (slack + 1)
    lengths = lengths.at[giver].add(-shifted).at[sink].add(shifted)
    labels = jnp.searchsorted(jnp.cumsum(lengths), jnp.arange(rows * top), side="right").astype(jnp.int32)
    table = labels.reshape(top, rows).T
    table = table[jax.random.permutation(jax.random.fold_in(own, 1), rows)]
    offset_by = jax.random.randint(jax.random.fold_in(own, 2), (rows, 1), 0, top)
    return jnp.take_along_axis(table, (jnp.arange(top)[None, :] + offset_by) % top, axis=1)


def load_shares(amount, total, bound, slope, full):
    weights = [(1 << 20) // math.isqrt(rank ** slope) + 1 for rank in range(1, amount + 1)]
    largest = bound if full else min(bound, max(-(-total // amount), total * weights[0] // sum(weights)))
    least = 1 if total - largest >= amount - 1 else 0
    holding, surplus = [largest] + [least] * (amount - 1), total - largest - least * (amount - 1)
    while surplus > 0:
        candidates = [i for i in range(1, amount) if holding[i] < largest] or [i for i in range(1, amount) if holding[i] < bound]
        mass, budget = sum([weights[i] for i in candidates]), surplus
        for i in candidates:
            addition = min(bound - holding[i], max(1, budget * weights[i] // mass), surplus)
            holding[i] = holding[i] + addition
            surplus = surplus - addition
    return np.array(holding)


def gaussian(key, shape, width, most, split=(), held_as=jnp.bfloat16):
    loudness = steps_of(key, shape, split, -0.22, 0.18) if split else 1.0
    array = jax.random.normal(key, shape, jnp.float32) * width * loudness
    return jnp.minimum(jnp.maximum(array, -most), most).astype(held_as)


def setup_inputs(seed: int = 0) -> dict:
    seeds = jax.random.split(jax.random.key(seed), 9)
    adjoint_flux = gaussian(seeds[0], (HOURS, FIELDS, OCELLS), 1.0, 6.0, ((2, 128),))
    ocean_wet = set_ends((jax.random.randint(seeds[1], (OCELLS,), 0, 4) < 3).astype(jnp.int32), jax.random.fold_in(seeds[1], 1), 0, 1)
    intersection_weight = gaussian(seeds[2], (NPAIRS, TOP, BLK, BLK), BLK ** -0.5, 0.5, ((0, 128),))
    pair_owner_keys = jax.random.split(jax.random.fold_in(seeds[3], 1), NPAIRS // OB)
    pair_owner_turns = jax.random.permutation(jax.random.fold_in(seeds[3], 3), NPAIRS // OB)
    pair_owner = jax.vmap(lambda own, number: assign_block(jax.random.fold_in(seeds[3], 2), own, number, OB, DEVICES, TOP, CAP, 2))(pair_owner_keys, pair_owner_turns).reshape((NPAIRS, TOP))
    pair_block = set_ends(jax.random.randint(seeds[4], (NPAIRS, TOP), 0, CB_DEV), jax.random.fold_in(seeds[4], 1), 0, CB_DEV - 1).astype(jnp.int32)
    land_sea = set_ends((jax.random.randint(seeds[5], (NLAT, NLON), 0, 3) < 2).astype(jnp.int32), jax.random.fold_in(seeds[5], 1), 0, 1)
    east_coef = jnp.clip(jnp.exp(math.log(0.24) - 2.0794415 * jax.random.uniform(seeds[6], (NLAT, NLON), jnp.float32) ** steps_of(seeds[6], (NLAT, NLON), ((0, 64), (1, 2)), -0.2, 0.2)), 0.03, 0.24)
    north_coef = jnp.clip(jnp.exp(math.log(0.24) - 2.0794415 * jax.random.uniform(seeds[7], (NLAT, NLON), jnp.float32) ** steps_of(seeds[7], (NLAT, NLON), ((0, 64), (1, 2)), -0.2, 0.2)), 0.03, 0.24)
    return dict(adjoint_flux=adjoint_flux, ocean_wet=ocean_wet, intersection_weight=intersection_weight, pair_owner=pair_owner, pair_block=pair_block, land_sea=land_sea, east_coef=east_coef, north_coef=north_coef)


def hour_weights(hours):
    frac = jnp.arange(hours, dtype=jnp.float32) / hours
    return jnp.stack([1.0 - frac, frac])


def smooth_global(field, east, north_open):
    east_flux = east * (jnp.roll(field, -1, axis=2) - field)
    above = jnp.concatenate([field[:, 1:], jnp.zeros_like(field[:, :1])], axis=1)
    north_flux = north_open * (above - field)
    below_flux = jnp.concatenate([jnp.zeros_like(north_flux[:, :1]), north_flux[:, :-1]], axis=1)
    return field + (east_flux - jnp.roll(east_flux, 1, axis=2)) + (north_flux - below_flux)


def reference(adjoint_flux, ocean_wet, intersection_weight, pair_owner, pair_block, land_sea, east_coef, north_coef):
    devices = N_TILE * N_SUB
    weights = hour_weights(HOURS)

    def one_device(total, index):
        start = index * (OB * BLK)
        flux = lax.dynamic_slice_in_dim(adjoint_flux, start, OB * BLK, 2).astype(jnp.float32)
        wet = lax.dynamic_slice_in_dim(ocean_wet, start, OB * BLK, 0).astype(jnp.float32)
        summed = jnp.zeros((2, FIELDS, OB * BLK), jnp.float32)
        for hour in range(HOURS):
            summed = summed + weights[:, hour][:, None, None] * flux[hour][None]
        timed = (summed * wet).reshape(CH, OB, BLK).astype(jnp.bfloat16)
        mats = lax.dynamic_slice_in_dim(intersection_weight, index * OB, OB, 0)
        contributions = jnp.einsum("hpo,pkoc->pkhc", timed.astype(jnp.float32), mats.astype(jnp.float32), precision=lax.Precision.HIGHEST)
        owners = lax.dynamic_slice_in_dim(pair_owner, index * OB, OB, 0)
        targets = lax.dynamic_slice_in_dim(pair_block, index * OB, OB, 0)
        slots = (owners * CB_DEV + targets).reshape(-1).astype(jnp.int32)
        total = total.at[slots].add(contributions.reshape(-1, CH, BLK))
        return total, None

    blocks, _ = lax.scan(one_device, jnp.zeros((devices * CB_DEV, CH, BLK), jnp.float32), jnp.arange(devices, dtype=jnp.int32))
    grid = blocks.reshape(N_TILE, N_SUB, LAT_DEV // 8, LON_DEV // LBW, CH, 8, LBW)
    grid = grid.transpose(4, 0, 2, 5, 1, 3, 6).reshape(CH, NLAT, NLON)
    field = grid * land_sea.astype(jnp.float32)
    north_open = jnp.where(jnp.arange(NLAT, dtype=jnp.int32)[:, None] < NLAT - 1, north_coef, jnp.float32(0.0))
    for turn in range(PASSES):
        field = smooth_global(field, east_coef, north_open)
    return field
```

```python
import functools

import jax
import jax.numpy as jnp
import numpy as np
from jax import lax
from jax.experimental import pallas as pl
from jax.experimental.pallas import tpu as pltpu
from jax.sharding import PartitionSpec as P

PASSES = 4
HALO = 4
CAP = 4
HOURS = 6
FIELDS = 7
BLK = 128
OB = 128
ROWS = 32
COLS = 720
ACROSS = 45
WIDE = 48
VR = ROWS + 8
VC = 768
DEV = 128
STRIDE = 37
W_CHUNKS = 8
F_CHUNKS = 4
MESH = pl.DeviceIdType.MESH
F32 = jnp.float32
BF16 = jnp.bfloat16


def iota(shape, dim):
    return lax.broadcasted_iota(jnp.int32, shape, dim)


def peer_of(tile, sub, j):
    o = (j * STRIDE) % DEV
    x = (tile // 16 + o // 32) % 4
    y = ((tile // 4) % 4 + (o // 8) % 4) % 4
    z = (sub * 2 + (tile // 2) % 2 + (o // 2) % 4) % 4
    c = (tile % 2 + o % 2) % 2
    return ((x * 4 + y) * 2 + z % 2) * 2 + c, z // 2


def swap_lanes_rows(x):
    s = iota(x.shape, 1)
    g = iota(x.shape, 2) // 16
    for m in (4, 2, 1):
        sb = (s // m) % 2
        gb = (g // m) % 2
        up = pltpu.roll(pltpu.roll(x, 16 * m, 2), 8 - m, 1)
        down = up if m == 4 else pltpu.roll(pltpu.roll(x, 128 - 16 * m, 2), m, 1)
        x = jnp.where(sb < gb, up, jnp.where(sb > gb, down, x))
    return x


def halo_start(v, count, tile, sub, row_out, row_in, col_out, col_in, cor_in, send, recv):
    low = iota((8, VC), 0) < HALO
    for i in range((count + 1) // 2):
        a, b = 2 * i, min(2 * i + 1, count - 1)
        row_out[0, i] = jnp.where(low, pltpu.roll(v[a, 24:32, :], 4, 0), v[b, 24:32, :])
        row_out[1, i] = jnp.where(low, v[a, 0:8, :], pltpu.roll(v[b, 0:8, :], 4, 0))
    lane = iota((ROWS, 128), 1)
    edge = jnp.zeros((ROWS, 128), F32)
    for f in range(count):
        left = v[f, 0:ROWS, 0:128]
        right = v[f, 0:ROWS, 640:768]
        if f:
            left = pltpu.roll(left, 8 * f, 1)
        right = pltpu.roll(right, (8 * f + 4 - 76) % 128, 1)
        edge = jnp.where((lane >= 8 * f) & (lane < 8 * f + 4), left, edge)
        edge = jnp.where((lane >= 8 * f + 4) & (lane < 8 * f + 8), right, edge)
    col_out[...] = edge
    up, down, other = (tile + 1) % 64, (tile + 63) % 64, 1 - sub
    n = (count + 1) // 2
    parts = (
        (row_out.at[0, pl.ds(0, n)], row_in.at[0, pl.ds(0, n)], (up, sub)),
        (row_out.at[1, pl.ds(0, n)], row_in.at[1, pl.ds(0, n)], (down, sub)),
        (col_out, col_in, (tile, other)),
        (col_out.at[pl.ds(24, 8)], cor_in.at[0], (up, other)),
        (col_out.at[pl.ds(0, 8)], cor_in.at[1], (down, other)),
    )
    copies = []
    for i, (src, dst, to) in enumerate(parts):
        copy = pltpu.make_async_remote_copy(
            src_ref=src,
            dst_ref=dst,
            send_sem=send.at[i],
            recv_sem=recv.at[i],
            device_id=to,
            device_id_type=MESH,
        )
        copy.start()
        copies.append(copy)
    return copies


def halo_finish(copies, v, count, row_in, col_in, cor_in):
    for copy in copies:
        copy.wait()
    low = iota((8, VC), 0) < HALO
    for i in range((count + 1) // 2):
        south, north = row_in[1, i], row_in[0, i]
        v[2 * i, ROWS:VR, :] = jnp.where(low, south, pltpu.roll(north, 4, 0))
        if 2 * i + 1 < count:
            v[2 * i + 1, ROWS:VR, :] = jnp.where(low, pltpu.roll(south, 4, 0), north)
    corner = jnp.where(iota((8, 128), 0) < HALO, cor_in[1], cor_in[0])
    edge = jnp.concatenate([col_in[...], corner], axis=0)
    lane = iota((VR, 128), 1)
    for f in range(count):
        own = v[f, :, 640:768]
        own = jnp.where((lane >= 80) & (lane < 84), pltpu.roll(edge, 80 - 8 * f, 1), own)
        own = jnp.where(lane >= 124, pltpu.roll(edge, 120 - 8 * f, 1), own)
        v[f, :, 640:768] = own


def kernel(
    flux_hbm,
    wet_hbm,
    w_hbm,
    owner_hbm,
    block_hbm,
    land_hbm,
    east_hbm,
    north_hbm,
    out_hbm,
    flux,
    wet,
    w,
    owner,
    block,
    land,
    east,
    north,
    items,
    index_v,
    index_s,
    labels,
    stage_a,
    stage_b,
    recv_a,
    recv_b,
    picked,
    grid_a,
    grid_b,
    coef,
    result,
    row_out,
    row_in,
    col_out,
    col_in,
    cor_in,
    in_sem,
    w_sem,
    f_sem,
    idx_sem,
    send_sem,
    recv_sem,
    halo_send,
    halo_recv,
    out_sem,
):
    tile, sub = lax.axis_index("tile"), lax.axis_index("sub")
    me = tile * 2 + sub

    small = []
    for i, (src, dst) in enumerate(
        (
            (owner_hbm, owner),
            (block_hbm, block),
            (wet_hbm, wet),
            (land_hbm, land),
            (east_hbm, east),
            (north_hbm, north),
        )
    ):
        copy = pltpu.make_async_copy(src, dst, in_sem.at[i])
        copy.start()
        small.append(copy)
    cells = OB * BLK // F_CHUNKS
    blocks = OB // W_CHUNKS
    flux_copies = [
        pltpu.make_async_copy(
            flux_hbm.at[:, :, pl.ds(i * cells, cells)],
            flux.at[:, :, pl.ds(i * cells, cells)],
            f_sem.at[i],
        )
        for i in range(F_CHUNKS)
    ]
    w_copies = [
        pltpu.make_async_copy(
            w_hbm.at[pl.ds(i * blocks, blocks)], w.at[pl.ds(i * blocks, blocks)], w_sem.at[i]
        )
        for i in range(W_CHUNKS)
    ]
    for i in range(W_CHUNKS):
        if i % (W_CHUNKS // F_CHUNKS) == 0:
            flux_copies[i // (W_CHUNKS // F_CHUNKS)].start()
        w_copies[i].start()

    barrier = pltpu.get_barrier_semaphore()

    def greet(i, carry):
        d = (me + i) % DEV
        pl.semaphore_signal(barrier, 1, device_id=(d // 2, d % 2), device_id_type=MESH)
        return carry

    lax.fori_loop(1, DEV, greet, 0)

    small[0].wait()
    small[1].wait()
    own = owner[...]
    blk = block[...]
    drow = iota((DEV, OB), 0)
    earlier = (iota((OB, OB), 0) < iota((OB, OB), 1)).astype(BF16)
    hit = [own[k : k + 1, :] == drow for k in range(2)]
    ones = [h.astype(F32) for h in hit]
    rank = [jnp.dot(o.astype(BF16), earlier, preferred_element_type=F32) for o in ones]
    rank[1] = rank[1] + jnp.sum(ones[0], axis=1, keepdims=True)
    wide = blk + (WIDE - ACROSS) * (
        (blk >= ACROSS).astype(jnp.int32)
        + (blk >= 2 * ACROSS).astype(jnp.int32)
        + (blk >= 3 * ACROSS).astype(jnp.int32)
    )
    wide = (wide + 1).astype(F32)
    position = iota((1, OB), 1).astype(F32) * 2.0
    first = iota((8, OB), 0)
    facts = []
    for k in range(2):
        facts.append(
            jnp.where(
                first == 0,
                wide[k : k + 1, :],
                jnp.where(first == 1, position + float(k - 2 * OB), 0.0),
            ).astype(BF16)
        )
    found = []
    for r in range(CAP):
        total = jnp.zeros((8, DEV), F32)
        for k in range(2):
            mine = jnp.where(rank[k] == float(r), ones[k], 0.0).astype(BF16)
            total = total + lax.dot_general(
                facts[k], mine, (((1,), (1,)), ((), ())), preferred_element_type=F32
            )
        found.append(total)
    row8 = iota((8, DEV), 0)
    index = jnp.zeros((8, DEV), F32)
    names = jnp.zeros((8, DEV), F32)
    for r in range(CAP):
        index = jnp.where(row8 == r, found[r][1:2, :] + float(2 * OB), index)
        names = jnp.where(row8 == r, found[r][0:1, :] - 1.0, names)
    index_v[...] = jnp.clip(index.astype(jnp.int32), 0, 2 * OB)
    to_smem = pltpu.make_async_copy(index_v, index_s, idx_sem)
    to_smem.start()
    labels[...] = jnp.concatenate([names, jnp.zeros((DEV - 8, DEV), F32)], axis=0).T

    coef[...] = jnp.zeros((2, VR, VC), F32)
    small[4].wait()
    small[5].wait()
    coef[0, 0:ROWS, 0:COLS] = east[...]
    row_global = tile * ROWS + iota((ROWS, COLS), 0)
    coef[1, 0:ROWS, 0:COLS] = jnp.where(row_global < 64 * ROWS - 1, north[...], 0.0)

    items[0, 2 * OB] = jnp.zeros((8, BLK), F32)
    items[1, 2 * OB] = jnp.zeros((8, BLK), F32)
    small[2].wait()
    frac = [np.float32(h) / np.float32(HOURS) for h in range(HOURS)]
    blank = jnp.zeros((1, BLK), F32)

    def contribute(p):
        at = pl.ds(pl.multiple_of(p * BLK, BLK), BLK)
        early = late = None
        for h in range(HOURS):
            x = flux[h, :, at].astype(F32)
            early = x if h == 0 else early + (np.float32(1.0) - frac[h]) * x
            if h:
                late = frac[h] * x if h == 1 else late + frac[h] * x
        mask = wet[pl.ds(p, 1), :].astype(F32)
        left = jnp.concatenate([early * mask, blank, late * mask, blank], axis=0).astype(BF16)
        for k in range(2):
            made = jnp.dot(left, w[p, k], preferred_element_type=F32)
            items[0, 2 * p + k] = made[0:8, :]
            items[1, 2 * p + k] = made[8:16, :]

    group = 8
    for i in range(W_CHUNKS):
        if i % (W_CHUNKS // F_CHUNKS) == 0:
            flux_copies[i // (W_CHUNKS // F_CHUNKS)].wait()
        w_copies[i].wait()

        def chunk(q, carry, i=i):
            for g in range(group):
                contribute(i * blocks + q * group + g)
            return carry

        lax.fori_loop(0, blocks // group, chunk, 0)

    to_smem.wait()
    pl.semaphore_wait(barrier, DEV - 1)

    coef_copies = halo_start(
        coef,
        2,
        tile,
        sub,
        row_out.at[0],
        row_in.at[0],
        col_out.at[0],
        col_in.at[0],
        cor_in.at[0],
        halo_send.at[0],
        halo_recv.at[0],
    )

    def pack(half, d, write):
        for r in range(CAP):
            write(r * FIELDS, items[half, index_s[r, d]][0:FIELDS, :])
        if half == 0:
            write(CAP * FIELDS, labels[pl.ds(d, 1), :])

    for half, stage, recv in ((0, stage_a, recv_a), (1, stage_b, recv_b)):

        def send(j, carry, half=half, stage=stage, recv=recv):
            t, u = peer_of(tile, sub, j)

            def write(row, value):
                stage[j, row : row + value.shape[0], :] = value

            pack(half, t * 2 + u, write)
            pltpu.make_async_remote_copy(
                src_ref=stage.at[j],
                dst_ref=recv.at[me],
                send_sem=send_sem.at[half],
                recv_sem=recv_sem.at[half],
                device_id=(t, u),
                device_id_type=MESH,
            ).start()
            return carry

        lax.fori_loop(1, DEV, send, 0)

    for half, recv in ((0, recv_a), (1, recv_b)):

        def write(row, value, recv=recv):
            recv[me, row : row + value.shape[0], :] = value

        pack(half, me, write)

    small[3].wait()
    halo_finish(coef_copies, coef, 2, row_in.at[0], col_in.at[0], cor_in.at[0])

    out_copies = []
    for half, stage, recv, grid in (
        (0, stage_a, recv_a, grid_a),
        (1, stage_b, recv_b, grid_b),
    ):
        everything = recv.at[pl.ds(0, DEV - 1)]
        pltpu.make_async_copy(everything, everything, recv_sem.at[half]).wait()
        if half == 0:
            named = recv[:, CAP * FIELDS, :].T
            rows = iota((4 * WIDE, DEV), 0).astype(F32)
            for r in range(CAP):
                picked[:, r * DEV : (r + 1) * DEV] = (rows == named[r : r + 1, :]).astype(BF16)
        for f in range(FIELDS):
            got = jnp.concatenate(
                [recv[:, r * FIELDS + f, :].astype(BF16) for r in range(CAP)], axis=0
            )
            sums = jnp.dot(picked[...], got, preferred_element_type=F32)
            tiles = swap_lanes_rows(sums.reshape(24, 8, 128))
            for r in range(4):
                for q in range(6):
                    at = slice(128 * q, 128 * q + 128)
                    value = tiles[6 * r + q]
                    if q < 5:
                        value = value * land[8 * r : 8 * r + 8, at].astype(F32)
                        grid[f, 8 * r : 8 * r + 8, at] = value
                    else:
                        sea = land[8 * r : 8 * r + 8, 640:720].astype(F32)
                        grid[f, 8 * r : 8 * r + 8, at] = value
                        grid[f, 8 * r : 8 * r + 8, 640:720] = value[:, 0:80] * sea
        copies = halo_start(
            grid,
            FIELDS,
            tile,
            sub,
            row_out.at[1 + half],
            row_in.at[1 + half],
            col_out.at[1 + half],
            col_in.at[1 + half],
            cor_in.at[1 + half],
            halo_send.at[1 + half],
            halo_recv.at[1 + half],
        )
        halo_finish(
            copies, grid, FIELDS, row_in.at[1 + half], col_in.at[1 + half], cor_in.at[1 + half]
        )

        def smooth(f, carry, grid=grid, half=half):
            v = grid[f]
            for turn in range(PASSES):
                flow = coef[0] * (pltpu.roll(v, VC - 1, 1) - v)
                rise = coef[1] * (pltpu.roll(v, VR - 1, 0) - v)
                v = v + (flow - pltpu.roll(flow, 1, 1)) + (rise - pltpu.roll(rise, 1, 0))
            result[half * FIELDS + f] = v[0:ROWS, 0:COLS]
            return carry

        lax.fori_loop(0, FIELDS, smooth, 0)
        span = pl.ds(half * FIELDS, FIELDS)
        copy = pltpu.make_async_copy(result.at[span], out_hbm.at[span], out_sem.at[half])
        copy.start()
        out_copies.append(copy)

    for half, stage in ((0, stage_a), (1, stage_b)):
        everything = stage.at[pl.ds(1, DEV - 1)]
        pltpu.make_async_copy(everything, everything, send_sem.at[half]).wait()
    for copy in out_copies:
        copy.wait()


def on_device(
    adjoint_flux,
    ocean_wet,
    intersection_weight,
    pair_owner,
    pair_block,
    land_sea,
    east_coef,
    north_coef,
):
    vmem = pltpu.VMEM
    dma = pltpu.SemaphoreType.DMA
    return pl.pallas_call(
        kernel,
        out_shape=jax.ShapeDtypeStruct((2 * FIELDS, ROWS, COLS), F32),
        in_specs=[pl.BlockSpec(memory_space=pl.ANY)] * 8,
        out_specs=pl.BlockSpec(memory_space=pl.ANY),
        scratch_shapes=[
            vmem((HOURS, FIELDS, OB * BLK), BF16),
            vmem((OB, BLK), jnp.int32),
            vmem((OB, 2, BLK, BLK), BF16),
            vmem((2, OB), jnp.int32),
            vmem((2, OB), jnp.int32),
            vmem((ROWS, COLS), jnp.int32),
            vmem((ROWS, COLS), F32),
            vmem((ROWS, COLS), F32),
            vmem((2, 2 * OB + 1, 8, BLK), F32),
            vmem((8, DEV), jnp.int32),
            pltpu.SMEM((8, DEV), jnp.int32),
            vmem((DEV, DEV), F32),
            vmem((DEV, CAP * FIELDS + 1, BLK), F32),
            vmem((DEV, CAP * FIELDS, BLK), F32),
            vmem((DEV, CAP * FIELDS + 1, BLK), F32),
            vmem((DEV, CAP * FIELDS, BLK), F32),
            vmem((4 * WIDE, CAP * DEV), BF16),
            vmem((FIELDS, VR, VC), F32),
            vmem((FIELDS, VR, VC), F32),
            vmem((2, VR, VC), F32),
            vmem((2 * FIELDS, ROWS, COLS), F32),
            vmem((3, 2, 4, 8, VC), F32),
            vmem((3, 2, 4, 8, VC), F32),
            vmem((3, ROWS, 128), F32),
            vmem((3, ROWS, 128), F32),
            vmem((3, 2, 8, 128), F32),
            dma((6,)),
            dma((W_CHUNKS,)),
            dma((F_CHUNKS,)),
            dma,
            dma((2,)),
            dma((2,)),
            dma((3, 5)),
            dma((3, 5)),
            dma((2,)),
        ],
        compiler_params=pltpu.CompilerParams(
            collective_id=0, has_side_effects=True, vmem_limit_bytes=60 * 2**20
        ),
        cost_estimate=pl.CostEstimate(
            flops=4 * 10**8, bytes_accessed=12 * 10**6, transcendentals=0
        ),
    )(
        adjoint_flux,
        ocean_wet.reshape(OB, BLK),
        intersection_weight,
        pair_owner.T,
        pair_block.T,
        land_sea,
        east_coef,
        north_coef,
    )


def solution(mesh):
    in_specs = (
        P(None, None, ("tile", "sub")),
        P(("tile", "sub")),
        P(("tile", "sub"), None, None, None),
        P(("tile", "sub"), None),
        P(("tile", "sub"), None),
        P("tile", "sub"),
        P("tile", "sub"),
        P("tile", "sub"),
    )
    out_specs = P(None, "tile", "sub")
    return jax.shard_map(
        on_device, mesh=mesh, in_specs=in_specs, out_specs=out_specs, check_vma=False
    )
```

```python
import functools

import jax
import jax.numpy as jnp
import numpy as np
from jax import lax
from jax.experimental import pallas as pl
from jax.experimental.pallas import tpu as pltpu
from jax.sharding import PartitionSpec as P

PASSES = 4
HALO = 4
CAP = 4
HOURS = 6
FIELDS = 7
PARTS = ((0, 8), (8, 6))
BLK = 128
OB = 128
ROWS = 32
COLS = 720
ACROSS = 45
WIDE = 48
VR = ROWS + 8
VC = 768
DEV = 128
STRIDE = 37
W_CHUNKS = 8
F_CHUNKS = 4
MESH = pl.DeviceIdType.MESH
F32 = jnp.float32
BF16 = jnp.bfloat16


def iota(shape, dim):
    return lax.broadcasted_iota(jnp.int32, shape, dim)


def peer_of(tile, sub, j):
    o = (j * STRIDE) % DEV
    x = (tile // 16 + o // 32) % 4
    y = ((tile // 4) % 4 + (o // 8) % 4) % 4
    z = (sub * 2 + (tile // 2) % 2 + (o // 2) % 4) % 4
    c = (tile % 2 + o % 2) % 2
    return ((x * 4 + y) * 2 + z % 2) * 2 + c, z // 2


def swap_vregs_rows(xs):
    s = iota((8, 128), 0)
    xs = list(xs)
    for m in (1, 2, 4):
        low = (s // m) % 2 == 0
        for a in range(8):
            if (a // m) % 2 == 0:
                p, q = xs[a], xs[a + m]
                xs[a] = jnp.where(low, p, pltpu.roll(q, m, 0))
                xs[a + m] = jnp.where(low, pltpu.roll(p, 8 - m, 0), q)
    return xs


def swap_vregs_lanes(xs):
    g = iota((8, 128), 1) // 16
    xs = list(xs)
    for m in (1, 2, 4):
        low = (g // m) % 2 == 0
        for a in range(8):
            if (a // m) % 2 == 0:
                p, q = xs[a], xs[a + m]
                xs[a] = jnp.where(low, p, pltpu.roll(q, 16 * m, 1))
                xs[a + m] = jnp.where(low, pltpu.roll(p, 128 - 16 * m, 1), q)
    return xs


def halo_start(v, tile, sub, col_out, col_in, cor_in, send, recv):
    lane = iota((8, 128), 1)
    for n in range(2):
        edge = jnp.zeros((8, 128), F32)
        for i in range(16):
            row = HALO + 16 * n + i
            left, right = v[row, :, 0:128], v[row, :, 640:768]
            if i:
                left = pltpu.roll(left, 8 * i, 1)
            right = pltpu.roll(right, (8 * i + 4 - 76) % 128, 1)
            edge = jnp.where((lane >= 8 * i) & (lane < 8 * i + 4), left, edge)
            edge = jnp.where((lane >= 8 * i + 4) & (lane < 8 * i + 8), right, edge)
        col_out[n] = edge
    up, down, other = (tile + 1) % 64, (tile + 63) % 64, 1 - sub
    parts = (
        (v.at[pl.ds(ROWS, HALO)], v.at[pl.ds(0, HALO)], (up, sub)),
        (v.at[pl.ds(HALO, HALO)], v.at[pl.ds(HALO + ROWS, HALO)], (down, sub)),
        (col_out, col_in, (tile, other)),
        (col_out.at[1], cor_in.at[0], (up, other)),
        (col_out.at[0], cor_in.at[1], (down, other)),
    )
    copies = []
    for i, (src, dst, to) in enumerate(parts):
        copy = pltpu.make_async_remote_copy(
            src_ref=src,
            dst_ref=dst,
            send_sem=send.at[i],
            recv_sem=recv.at[i],
            device_id=to,
            device_id_type=MESH,
        )
        copy.start()
        copies.append(copy)
    return copies


def halo_finish(copies, v, col_in, cor_in):
    for copy in copies:
        copy.wait()
    lane = iota((8, 128), 1)
    for row in range(VR):
        i = row - HALO
        if i < 0:
            edge, off = cor_in[0], 8 * ((ROWS + i) % 16)
        elif i >= ROWS:
            edge, off = cor_in[1], 8 * (i - ROWS)
        else:
            edge, off = col_in[i // 16], 8 * (i % 16)
        own = v[row, :, 640:768]
        after = pltpu.roll(edge, (80 - off) % 128, 1)
        before = pltpu.roll(edge, (120 - off) % 128, 1)
        own = jnp.where((lane >= 80) & (lane < 84), after, jnp.where(lane >= 124, before, own))
        v[row, :, 640:768] = own


def kernel(
    flux_hbm,
    wet_hbm,
    w_hbm,
    owner_hbm,
    block_hbm,
    land_hbm,
    east_hbm,
    north_hbm,
    out_hbm,
    flux,
    wet,
    w,
    owner,
    block,
    land,
    east,
    north,
    items,
    index_v,
    index_s,
    labels,
    stage_a,
    stage_b,
    recv_a,
    recv_b,
    picked,
    sums,
    padded,
    grid_a,
    grid_b,
    coef,
    east_b,
    north_b,
    result,
    col_out,
    col_in,
    cor_in,
    in_sem,
    w_sem,
    f_sem,
    idx_sem,
    send_sem,
    recv_sem,
    halo_send,
    halo_recv,
    out_sem,
):
    tile, sub = lax.axis_index("tile"), lax.axis_index("sub")
    me = tile * 2 + sub

    small = []
    for i, (src, dst) in enumerate(
        (
            (owner_hbm, owner),
            (block_hbm, block),
            (wet_hbm, wet),
            (land_hbm, land),
            (east_hbm, east),
            (north_hbm, north),
        )
    ):
        copy = pltpu.make_async_copy(src, dst, in_sem.at[i])
        copy.start()
        small.append(copy)
    cells = OB * BLK // F_CHUNKS
    blocks = OB // W_CHUNKS
    flux_copies = [
        pltpu.make_async_copy(
            flux_hbm.at[:, :, pl.ds(i * cells, cells)],
            flux.at[:, :, pl.ds(i * cells, cells)],
            f_sem.at[i],
        )
        for i in range(F_CHUNKS)
    ]
    w_copies = [
        pltpu.make_async_copy(
            w_hbm.at[pl.ds(i * blocks, blocks)], w.at[pl.ds(i * blocks, blocks)], w_sem.at[i]
        )
        for i in range(W_CHUNKS)
    ]
    for i in range(W_CHUNKS):
        if i % (W_CHUNKS // F_CHUNKS) == 0:
            flux_copies[i // (W_CHUNKS // F_CHUNKS)].start()
        w_copies[i].start()

    barrier = pltpu.get_barrier_semaphore()

    def greet(i, carry):
        d = (me + i) % DEV
        pl.semaphore_signal(barrier, 1, device_id=(d // 2, d % 2), device_id_type=MESH)
        return carry

    lax.fori_loop(1, DEV, greet, 0)

    small[0].wait()
    small[1].wait()
    own = owner[...]
    blk = block[...]
    drow = iota((DEV, OB), 0)
    earlier = (iota((OB, OB), 0) < iota((OB, OB), 1)).astype(BF16)
    hit = [own[k : k + 1, :] == drow for k in range(2)]
    ones = [h.astype(F32) for h in hit]
    rank = [jnp.dot(o.astype(BF16), earlier, preferred_element_type=F32) for o in ones]
    rank[1] = rank[1] + jnp.sum(ones[0], axis=1, keepdims=True)
    wide = blk + (WIDE - ACROSS) * (
        (blk >= ACROSS).astype(jnp.int32)
        + (blk >= 2 * ACROSS).astype(jnp.int32)
        + (blk >= 3 * ACROSS).astype(jnp.int32)
    )
    wide = (wide + 1).astype(F32)
    position = iota((1, OB), 1).astype(F32) * 2.0
    first = iota((8, OB), 0)
    facts = []
    for k in range(2):
        facts.append(
            jnp.where(
                first == 0,
                wide[k : k + 1, :],
                jnp.where(first == 1, position + float(k - 2 * OB), 0.0),
            ).astype(BF16)
        )
    found = []
    for r in range(CAP):
        total = jnp.zeros((8, DEV), F32)
        for k in range(2):
            mine = jnp.where(rank[k] == float(r), ones[k], 0.0).astype(BF16)
            total = total + lax.dot_general(
                facts[k], mine, (((1,), (1,)), ((), ())), preferred_element_type=F32
            )
        found.append(total)
    row8 = iota((8, DEV), 0)
    index = jnp.zeros((8, DEV), F32)
    names = jnp.zeros((8, DEV), F32)
    for r in range(CAP):
        index = jnp.where(row8 == r, found[r][1:2, :] + float(2 * OB), index)
        names = jnp.where(row8 == r, found[r][0:1, :] - 1.0, names)
    index_v[...] = jnp.clip(index.astype(jnp.int32), 0, 2 * OB)
    to_smem = pltpu.make_async_copy(index_v, index_s, idx_sem)
    to_smem.start()
    labels[...] = jnp.concatenate([names, jnp.zeros((DEV - 8, DEV), F32)], axis=0).T

    padded[:, :, 640:VC] = jnp.zeros((3, ROWS, 128), F32)
    small[4].wait()
    small[5].wait()
    padded[0, :, 0:COLS] = east[...]
    row_global = tile * ROWS + iota((ROWS, COLS), 0)
    padded[1, :, 0:COLS] = jnp.where(row_global < 64 * ROWS - 1, north[...], 0.0)
    top = iota((8, VC), 0) == 0

    def lay(r, carry):
        at = pl.ds(pl.multiple_of(r * 8, 8), 8)
        ease, norse = padded[0, at, :], padded[1, at, :]
        for i in range(8):
            coef[HALO + 8 * r + i] = jnp.where(top, ease[i : i + 1, :], norse[i : i + 1, :])
        return carry

    lax.fori_loop(0, ROWS // 8, lay, 0)

    items[0, 2 * OB] = jnp.zeros((8, BLK), F32)
    items[1, 2 * OB] = jnp.zeros((8, BLK), F32)
    small[2].wait()
    frac = [np.float32(h) / np.float32(HOURS) for h in range(HOURS)]
    blank = jnp.zeros((1, BLK), F32)

    def contribute(p):
        at = pl.ds(pl.multiple_of(p * BLK, BLK), BLK)
        early = late = None
        for h in range(HOURS):
            x = flux[h, :, at].astype(F32)
            early = x if h == 0 else early + (np.float32(1.0) - frac[h]) * x
            if h:
                late = frac[h] * x if h == 1 else late + frac[h] * x
        mask = wet[pl.ds(p, 1), :].astype(F32)
        left = jnp.concatenate([early * mask, late * mask, blank, blank], axis=0).astype(BF16)
        for k in range(2):
            made = jnp.dot(left, w[p, k], preferred_element_type=F32)
            items[0, 2 * p + k] = made[0:8, :]
            items[1, 2 * p + k] = made[8:16, :]

    group = 8
    for i in range(W_CHUNKS):
        if i % (W_CHUNKS // F_CHUNKS) == 0:
            flux_copies[i // (W_CHUNKS // F_CHUNKS)].wait()
        w_copies[i].wait()

        def chunk(q, carry, i=i):
            for g in range(group):
                contribute(i * blocks + q * group + g)
            return carry

        lax.fori_loop(0, blocks // group, chunk, 0)

    to_smem.wait()
    pl.semaphore_wait(barrier, DEV - 1)

    coef_copies = halo_start(
        coef, tile, sub, col_out.at[0], col_in.at[0], cor_in.at[0], halo_send.at[0], halo_recv.at[0]
    )

    def pack(half, d, write):
        count = PARTS[half][1]
        for r in range(CAP):
            write(r * count, items[half, index_s[r, d]][0:count, :])
        if half == 0:
            write(CAP * count, labels[pl.ds(d, 1), :])

    for half, stage, recv in ((0, stage_a, recv_a), (1, stage_b, recv_b)):

        def send(j, carry, half=half, stage=stage, recv=recv):
            t, u = peer_of(tile, sub, j)

            def write(row, value):
                stage[j, row : row + value.shape[0], :] = value

            pack(half, t * 2 + u, write)
            pltpu.make_async_remote_copy(
                src_ref=stage.at[j],
                dst_ref=recv.at[me],
                send_sem=send_sem.at[half],
                recv_sem=recv_sem.at[half],
                device_id=(t, u),
                device_id_type=MESH,
            ).start()
            return carry

        lax.fori_loop(1, DEV, send, 0)

    for half, recv in ((0, recv_a), (1, recv_b)):

        def write(row, value, recv=recv):
            recv[me, row : row + value.shape[0], :] = value

        pack(half, me, write)

    small[3].wait()
    padded[2, :, 0:COLS] = land[...].astype(F32)
    halo_finish(coef_copies, coef, col_in.at[0], cor_in.at[0])

    def spread(i, carry):
        both = coef[i]
        east_b[i] = jnp.broadcast_to(both[0:1, :], (8, VC))
        north_b[i] = jnp.broadcast_to(both[1:2, :], (8, VC))
        return carry

    lax.fori_loop(0, VR, spread, 0)

    def assemble(half, recv, grid):
        count = PARTS[half][1]
        everything = recv.at[pl.ds(0, DEV - 1)]
        pltpu.make_async_copy(everything, everything, recv_sem.at[half]).wait()
        if half == 0:
            named = recv[:, CAP * count, :].T
            rows = iota((4 * WIDE, DEV), 0).astype(F32)
            for r in range(CAP):
                picked[:, r * DEV : (r + 1) * DEV] = (rows == named[r : r + 1, :]).astype(BF16)
        for f in range(0, count, 2):
            got = jnp.concatenate(
                [
                    jnp.concatenate(
                        [recv[:, r * count + f + e, :].astype(BF16) for r in range(CAP)], axis=0
                    )
                    for e in range(2)
                ],
                axis=1,
            )
            both = jnp.dot(picked[...], got, preferred_element_type=F32)
            sums[f] = both[:, 0:128]
            sums[f + 1] = both[:, 128:256]
        none = jnp.zeros((8, 128), F32)

        def place(r, carry):
            for q in range(6):
                lanes = slice(128 * q, 128 * q + 128)
                at = pl.ds(pl.multiple_of(r * WIDE + 8 * q, 8), 8)
                xs = [sums[f, at, :] if f < count else none for f in range(8)]
                xs = swap_vregs_lanes(swap_vregs_rows(xs))
                sea = padded[2, pl.ds(pl.multiple_of(r * 8, 8), 8), lanes]
                for i in range(8):
                    grid[HALO + 8 * r + i, :, lanes] = xs[i] * sea[i : i + 1, :]
            return carry

        lax.fori_loop(0, ROWS // 8, place, 0)
        return halo_start(
            grid,
            tile,
            sub,
            col_out.at[1 + half],
            col_in.at[1 + half],
            cor_in.at[1 + half],
            halo_send.at[1 + half],
            halo_recv.at[1 + half],
        )

    def smooth(half, copies, grid):
        start, count = PARTS[half]
        halo_finish(copies, grid, col_in.at[1 + half], cor_in.at[1 + half])
        for turn in range(PASSES):
            low, high = turn + 1, VR - 1 - turn
            v = grid[low]
            below = north_b[low - 1] * (v - grid[low - 1])

            def line(i, carry):
                v, below = carry
                above = grid[i + 1]
                rise = north_b[i] * (above - v)
                flow = east_b[i] * (pltpu.roll(v, VC - 1, 1) - v)
                grid[i] = v + (flow - pltpu.roll(flow, 1, 1)) + (rise - below)
                return above, rise

            lax.fori_loop(low, high, line, (v, below))

        def turn_back(r, carry):
            for q in range(6):
                lanes = slice(128 * q, min(128 * q + 128, COLS))
                xs = [grid[HALO + 8 * r + i, :, 128 * q : 128 * q + 128] for i in range(8)]
                xs = swap_vregs_rows(xs)
                for c in range(count):
                    result[start + c, pl.ds(pl.multiple_of(r * 8, 8), 8), lanes] = xs[c][
                        :, 0 : min(128, COLS - 128 * q)
                    ]
            return carry

        lax.fori_loop(0, ROWS // 8, turn_back, 0)
        span = pl.ds(start, count)
        copy = pltpu.make_async_copy(result.at[span], out_hbm.at[span], out_sem.at[half])
        copy.start()
        return copy

    halo_a = assemble(0, recv_a, grid_a)
    halo_b = assemble(1, recv_b, grid_b)
    out_a = smooth(0, halo_a, grid_a)
    out_b = smooth(1, halo_b, grid_b)

    for half, stage in ((0, stage_a), (1, stage_b)):
        everything = stage.at[pl.ds(1, DEV - 1)]
        pltpu.make_async_copy(everything, everything, send_sem.at[half]).wait()
    out_a.wait()
    out_b.wait()


def on_device(
    adjoint_flux,
    ocean_wet,
    intersection_weight,
    pair_owner,
    pair_block,
    land_sea,
    east_coef,
    north_coef,
):
    vmem = pltpu.VMEM
    dma = pltpu.SemaphoreType.DMA
    return pl.pallas_call(
        kernel,
        out_shape=jax.ShapeDtypeStruct((2 * FIELDS, ROWS, COLS), F32),
        in_specs=[pl.BlockSpec(memory_space=pl.ANY)] * 8,
        out_specs=pl.BlockSpec(memory_space=pl.ANY),
        scratch_shapes=[
            vmem((HOURS, FIELDS, OB * BLK), BF16),
            vmem((OB, BLK), jnp.int32),
            vmem((OB, 2, BLK, BLK), BF16),
            vmem((2, OB), jnp.int32),
            vmem((2, OB), jnp.int32),
            vmem((ROWS, COLS), jnp.int32),
            vmem((ROWS, COLS), F32),
            vmem((ROWS, COLS), F32),
            vmem((2, 2 * OB + 1, 8, BLK), F32),
            vmem((8, DEV), jnp.int32),
            pltpu.SMEM((8, DEV), jnp.int32),
            vmem((DEV, DEV), F32),
            vmem((DEV, CAP * PARTS[0][1] + 1, BLK), F32),
            vmem((DEV, CAP * PARTS[1][1], BLK), F32),
            vmem((DEV, CAP * PARTS[0][1] + 1, BLK), F32),
            vmem((DEV, CAP * PARTS[1][1], BLK), F32),
            vmem((4 * WIDE, CAP * DEV), BF16),
            vmem((8, 4 * WIDE, 128), F32),
            vmem((3, ROWS, VC), F32),
            vmem((VR, 8, VC), F32),
            vmem((VR, 8, VC), F32),
            vmem((VR, 8, VC), F32),
            vmem((VR, 8, VC), F32),
            vmem((VR, 8, VC), F32),
            vmem((2 * FIELDS, ROWS, COLS), F32),
            vmem((3, 2, 8, 128), F32),
            vmem((3, 2, 8, 128), F32),
            vmem((3, 2, 8, 128), F32),
            dma((6,)),
            dma((W_CHUNKS,)),
            dma((F_CHUNKS,)),
            dma,
            dma((2,)),
            dma((2,)),
            dma((3, 5)),
            dma((3, 5)),
            dma((2,)),
        ],
        compiler_params=pltpu.CompilerParams(
            collective_id=0, has_side_effects=True, vmem_limit_bytes=60 * 2**20
        ),
        cost_estimate=pl.CostEstimate(
            flops=4 * 10**8, bytes_accessed=12 * 10**6, transcendentals=0
        ),
    )(
        adjoint_flux,
        ocean_wet.reshape(OB, BLK),
        intersection_weight,
        pair_owner.T,
        pair_block.T,
        land_sea,
        east_coef,
        north_coef,
    )


def solution(mesh):
    in_specs = (
        P(None, None, ("tile", "sub")),
        P(("tile", "sub")),
        P(("tile", "sub"), None, None, None),
        P(("tile", "sub"), None),
        P(("tile", "sub"), None),
        P("tile", "sub"),
        P("tile", "sub"),
        P("tile", "sub"),
    )
    out_specs = P(None, "tile", "sub")
    return jax.shard_map(
        on_device, mesh=mesh, in_specs=in_specs, out_specs=out_specs, check_vma=False
    )
```

```python
import functools

import jax
import jax.numpy as jnp
import numpy as np
from jax import lax
from jax.experimental import pallas as pl
from jax.experimental.pallas import tpu as pltpu
from jax.sharding import PartitionSpec as P

PASSES = 4
HALO = 4
CAP = 4
GROUPS = 4
EACH = 32
HOURS = 6
FIELDS = 7
CH = 14
PARTS = ((0, 8), (8, 6))
BLK = 128
OB = 128
ROWS = 32
COLS = 720
ACROSS = 45
WIDE = 48
VR = ROWS + 8
VC = 768
DEV = 128
STRIDE = 37
W_CHUNKS = 8
F_CHUNKS = 8
MESH = pl.DeviceIdType.MESH
F32 = jnp.float32
BF16 = jnp.bfloat16


def iota(shape, dim):
    return lax.broadcasted_iota(jnp.int32, shape, dim)


def peer_of(tile, sub, j):
    o = (j * STRIDE) % DEV
    x = (tile // 16 + o // 32) % 4
    y = ((tile // 4) % 4 + (o // 8) % 4) % 4
    z = (sub * 2 + (tile // 2) % 2 + (o // 2) % 4) % 4
    c = (tile % 2 + o % 2) % 2
    return ((x * 4 + y) * 2 + z % 2) * 2 + c, z // 2


def swap_vregs_rows(xs):
    s = iota((8, 128), 0)
    xs = list(xs)
    for m in (1, 2, 4):
        low = (s // m) % 2 == 0
        for a in range(8):
            if (a // m) % 2 == 0:
                p, q = xs[a], xs[a + m]
                xs[a] = jnp.where(low, p, pltpu.roll(q, m, 0))
                xs[a + m] = jnp.where(low, pltpu.roll(p, 8 - m, 0), q)
    return xs


def swap_vregs_lanes(xs):
    g = iota((8, 128), 1) // 16
    xs = list(xs)
    for m in (1, 2, 4):
        low = (g // m) % 2 == 0
        for a in range(8):
            if (a // m) % 2 == 0:
                p, q = xs[a], xs[a + m]
                xs[a] = jnp.where(low, p, pltpu.roll(q, 16 * m, 1))
                xs[a + m] = jnp.where(low, pltpu.roll(p, 128 - 16 * m, 1), q)
    return xs


def gather_edges(v, col_out):
    lane = iota((8, 128), 1)
    for n in range(2):
        edge = jnp.zeros((8, 128), F32)
        for i in range(16):
            row = HALO + 16 * n + i
            left, right = v[row, :, 0:128], v[row, :, 640:768]
            if i:
                left = pltpu.roll(left, 8 * i, 1)
            right = pltpu.roll(right, (8 * i + 4 - 76) % 128, 1)
            edge = jnp.where((lane >= 8 * i) & (lane < 8 * i + 4), left, edge)
            edge = jnp.where((lane >= 8 * i + 4) & (lane < 8 * i + 8), right, edge)
        col_out[n] = edge


def halo_start(v, ready, tile, sub, col_out, col_in, cor_in, send, recv):
    up, down, other = (tile + 1) % 64, (tile + 63) % 64, 1 - sub
    parts = (
        (v.at[pl.ds(ROWS, HALO)], v.at[pl.ds(0, HALO)], (up, sub)),
        (v.at[pl.ds(HALO, HALO)], v.at[pl.ds(HALO + ROWS, HALO)], (down, sub)),
        (col_out, col_in, (tile, other)),
        (col_out.at[1], cor_in.at[0], (up, other)),
        (col_out.at[0], cor_in.at[1], (down, other)),
    )
    copies = []
    for i, (src, dst, to) in enumerate(parts):
        if i == 2 and not ready:
            gather_edges(v, col_out)
        copy = pltpu.make_async_remote_copy(
            src_ref=src,
            dst_ref=dst,
            send_sem=send.at[i],
            recv_sem=recv.at[i],
            device_id=to,
            device_id_type=MESH,
        )
        copy.start()
        copies.append(copy)
    return copies


def halo_finish(copies, v, col_in, cor_in):
    for copy in copies:
        copy.wait()
    lane = iota((8, 128), 1)
    for row in range(VR):
        i = row - HALO
        if i < 0:
            edge, off = cor_in[0], 8 * ((ROWS + i) % 16)
        elif i >= ROWS:
            edge, off = cor_in[1], 8 * (i - ROWS)
        else:
            edge, off = col_in[i // 16], 8 * (i % 16)
        own = v[row, :, 640:768]
        after = pltpu.roll(edge, (80 - off) % 128, 1)
        before = pltpu.roll(edge, (120 - off) % 128, 1)
        own = jnp.where((lane >= 80) & (lane < 84), after, jnp.where(lane >= 124, before, own))
        v[row, :, 640:768] = own


def kernel(
    flux_hbm,
    wet_hbm,
    w_hbm,
    owner_hbm,
    block_hbm,
    land_hbm,
    east_hbm,
    north_hbm,
    out_hbm,
    flux,
    wet,
    w,
    owner,
    block,
    land,
    east,
    north,
    items,
    index_v,
    index_s,
    labels,
    stage,
    recv,
    sums,
    padded,
    grid_a,
    grid_b,
    coef,
    east_b,
    west_b,
    north_b,
    spare,
    result,
    col_out,
    col_in,
    cor_in,
    in_sem,
    w_sem,
    f_sem,
    idx_sem,
    send_sem,
    recv_sem,
    halo_send,
    halo_recv,
    out_sem,
):
    tile, sub = lax.axis_index("tile"), lax.axis_index("sub")
    me = tile * 2 + sub

    small = []
    for i, (src, dst) in enumerate(
        (
            (owner_hbm, owner),
            (block_hbm, block),
            (wet_hbm, wet),
            (land_hbm, land),
            (east_hbm, east),
            (north_hbm, north),
        )
    ):
        copy = pltpu.make_async_copy(src, dst, in_sem.at[i])
        copy.start()
        small.append(copy)
    blocks = OB // W_CHUNKS
    cells = blocks * BLK

    def bring(i):
        at = pl.ds(pl.multiple_of(i * cells, cells), cells)
        ocean = pl.ds(i * blocks, blocks)
        return (
            pltpu.make_async_copy(flux_hbm.at[:, :, at], flux.at[:, :, at], f_sem.at[i]),
            pltpu.make_async_copy(w_hbm.at[ocean], w.at[ocean], w_sem.at[i]),
        )

    for i in range(W_CHUNKS):
        for copy in bring(i):
            copy.start()

    barrier = pltpu.get_barrier_semaphore()

    def greet(i, carry):
        d = (me + i) % DEV
        pl.semaphore_signal(barrier, 1, device_id=(d // 2, d % 2), device_id_type=MESH)
        return carry

    lax.fori_loop(1, DEV, greet, 0)

    small[0].wait()
    small[1].wait()
    own = owner[...]
    blk = block[...]
    drow = iota((DEV, OB), 0)
    earlier = (iota((OB, OB), 0) < iota((OB, OB), 1)).astype(BF16)
    hit = [own[k : k + 1, :] == drow for k in range(2)]
    ones = [h.astype(F32) for h in hit]
    rank = [jnp.dot(o.astype(BF16), earlier, preferred_element_type=F32) for o in ones]
    rank[1] = rank[1] + jnp.sum(ones[0], axis=1, keepdims=True)
    wide = blk + (WIDE - ACROSS) * (
        (blk >= ACROSS).astype(jnp.int32)
        + (blk >= 2 * ACROSS).astype(jnp.int32)
        + (blk >= 3 * ACROSS).astype(jnp.int32)
    )
    wide = (wide + 1).astype(F32)
    position = iota((1, OB), 1).astype(F32) * 2.0
    first = iota((8, OB), 0)
    facts = []
    for k in range(2):
        facts.append(
            jnp.where(
                first == 0,
                wide[k : k + 1, :],
                jnp.where(first == 1, position + float(k - 2 * OB), 0.0),
            ).astype(BF16)
        )
    found = []
    for r in range(CAP):
        total = jnp.zeros((8, DEV), F32)
        for k in range(2):
            mine = jnp.where(rank[k] == float(r), ones[k], 0.0).astype(BF16)
            total = total + lax.dot_general(
                facts[k], mine, (((1,), (1,)), ((), ())), preferred_element_type=F32
            )
        found.append(total)
    row8 = iota((8, DEV), 0)
    index = jnp.zeros((8, DEV), F32)
    names = jnp.zeros((8, DEV), F32)
    for r in range(CAP):
        index = jnp.where(row8 == r, found[r][1:2, :] + float(2 * OB), index)
        names = jnp.where(row8 == r, found[r][0:1, :] - 1.0, names)
    index_v[...] = jnp.clip(index.astype(jnp.int32), 0, 2 * OB)
    to_smem = pltpu.make_async_copy(index_v, index_s, idx_sem)
    to_smem.start()
    labels[...] = jnp.concatenate([names, jnp.zeros((DEV - 8, DEV), F32)], axis=0).T

    padded[:, :, 640:VC] = jnp.zeros((3, ROWS, 128), F32)
    small[4].wait()
    small[5].wait()
    padded[0, :, 0:COLS] = east[...]
    row_global = tile * ROWS + iota((ROWS, COLS), 0)
    padded[1, :, 0:COLS] = jnp.where(row_global < 64 * ROWS - 1, north[...], 0.0)
    top = iota((8, VC), 0) == 0

    def lay(r, carry):
        at = pl.ds(pl.multiple_of(r * 8, 8), 8)
        ease, norse = padded[0, at, :], padded[1, at, :]
        for i in range(8):
            coef[HALO + 8 * r + i] = jnp.where(top, ease[i : i + 1, :], norse[i : i + 1, :])
        return carry

    lax.fori_loop(0, ROWS // 8, lay, 0)

    gather_edges(coef, col_out.at[0])

    items[0, 2 * OB] = jnp.zeros((8, BLK), F32)
    items[1, 2 * OB] = jnp.zeros((8, BLK), F32)
    small[2].wait()
    frac = [np.float32(h) / np.float32(HOURS) for h in range(HOURS)]
    blank = jnp.zeros((1, BLK), F32)

    def timed(p):
        at = pl.ds(pl.multiple_of(p * BLK, BLK), BLK)
        early = late = None
        for h in range(HOURS):
            x = flux[h, :, at].astype(F32)
            early = x if h == 0 else early + (np.float32(1.0) - frac[h]) * x
            if h:
                late = frac[h] * x if h == 1 else late + frac[h] * x
        mask = wet[pl.ds(p, 1), :].astype(F32)
        return jnp.concatenate([early * mask, late * mask, blank, blank], axis=0).astype(BF16)

    nothing = jnp.zeros((16, BLK), BF16)

    def chunk(i, carry):
        for copy in bring(i):
            copy.wait()
        for g in range(0, blocks, 2):
            p = i * blocks + g
            left = jnp.concatenate(
                [
                    jnp.concatenate([timed(p), nothing], axis=1),
                    jnp.concatenate([nothing, timed(p + 1)], axis=1),
                ],
                axis=0,
            )
            right = jnp.concatenate(
                [jnp.concatenate([w[p + e, 0], w[p + e, 1]], axis=1) for e in range(2)], axis=0
            )
            made = jnp.dot(left, right, preferred_element_type=F32)
            for e in range(2):
                for k in range(2):
                    for half in range(2):
                        items[half, 2 * (p + e) + k] = made[
                            16 * e + 8 * half : 16 * e + 8 * half + 8, BLK * k : BLK * k + BLK
                        ]
        return carry

    lax.fori_loop(0, W_CHUNKS, chunk, 0)

    to_smem.wait()
    pl.semaphore_wait(barrier, DEV - 1)

    coef_copies = halo_start(
        coef, True, tile, sub, col_out.at[0], col_in.at[0], cor_in.at[0], halo_send.at[0], halo_recv.at[0]
    )

    def pack(d, into):
        for r in range(CAP):
            at = index_s[r, d]
            for half, (start, count) in enumerate(PARTS):
                row = r * CH + start
                into[row : row + count, :] = items[half, at][0:count, :]
        into[CAP * CH : CAP * CH + 1, :] = labels[pl.ds(d, 1), :]

    for g in range(GROUPS):

        def send(j, carry, g=g):
            t, u = peer_of(tile, sub, j)
            pack(t * 2 + u, stage.at[j])
            pltpu.make_async_remote_copy(
                src_ref=stage.at[j],
                dst_ref=recv.at[j],
                send_sem=send_sem,
                recv_sem=recv_sem.at[g],
                device_id=(t, u),
                device_id_type=MESH,
            ).start()
            return carry

        lax.fori_loop(max(1, EACH * g), EACH * (g + 1), send, 0)

    pack(me, recv.at[0])

    small[3].wait()
    padded[2, :, 0:COLS] = land[...].astype(F32)
    slot_rows = iota((4 * WIDE, CAP * EACH), 0).astype(F32)

    def add_group(g):
        low = max(1, EACH * g)
        everything = recv.at[pl.ds(low, EACH * (g + 1) - low)]
        pltpu.make_async_copy(everything, everything, recv_sem.at[g]).wait()
        here = slice(EACH * g, EACH * (g + 1))
        named = recv[here, CAP * CH, :].T
        line = jnp.concatenate([named[r : r + 1, :] for r in range(CAP)], axis=1)
        picked = (slot_rows == line).astype(BF16)
        for f in range(0, CH, 2):
            got = jnp.concatenate(
                [
                    jnp.concatenate(
                        [recv[here, r * CH + f + e, :].astype(BF16) for r in range(CAP)], axis=0
                    )
                    for e in range(2)
                ],
                axis=1,
            )
            both = jnp.dot(picked, got, preferred_element_type=F32)
            for e in range(2):
                part = both[:, 128 * e : 128 * e + 128]
                sums[f + e] = part if g == 0 else sums[f + e] + part

    def assemble(half, grid):
        start, count = PARTS[half]
        none = jnp.zeros((8, 128), F32)

        def place(r, carry):
            for q in range(6):
                lanes = slice(128 * q, 128 * q + 128)
                at = pl.ds(pl.multiple_of(r * WIDE + 8 * q, 8), 8)
                xs = [sums[start + f, at, :] if f < count else none for f in range(8)]
                xs = swap_vregs_lanes(swap_vregs_rows(xs))
                sea = padded[2, pl.ds(pl.multiple_of(r * 8, 8), 8), lanes]
                for i in range(8):
                    grid[HALO + 8 * r + i, :, lanes] = xs[i] * sea[i : i + 1, :]
            return carry

        lax.fori_loop(0, ROWS // 8, place, 0)
        return halo_start(
            grid,
            False,
            tile,
            sub,
            col_out.at[1 + half],
            col_in.at[1 + half],
            cor_in.at[1 + half],
            halo_send.at[1 + half],
            halo_recv.at[1 + half],
        )

    def smooth(half, copies, grid):
        start, count = PARTS[half]
        halo_finish(copies, grid, col_in.at[1 + half], cor_in.at[1 + half])
        def lines(src, dst, base, n):
            v = src[base]
            below = north_b[base - 1] * (v - src[base - 1])
            for k in range(n):
                at = base + k
                above = src[at + 1]
                rise = north_b[at] * (above - v)
                east_side = east_b[at] * (pltpu.roll(v, VC - 1, 1) - v)
                west_side = west_b[at] * (v - pltpu.roll(v, 1, 1))
                dst[at] = v + (east_side - west_side) + (rise - below)
                v, below = above, rise

        for turn in range(PASSES):
            src, dst = (grid, spare) if turn % 2 == 0 else (spare, grid)
            low, count_rows = turn + 1, VR - 2 - 2 * turn

            def block_of(n, carry, src=src, dst=dst, low=low):
                lines(src, dst, low + 8 * n, 8)
                return carry

            lax.fori_loop(0, count_rows // 8, block_of, 0)
            if count_rows % 8:
                lines(src, dst, low + count_rows // 8 * 8, count_rows % 8)

        def turn_back(r, carry):
            for q in range(6):
                lanes = slice(128 * q, min(128 * q + 128, COLS))
                xs = [grid[HALO + 8 * r + i, :, 128 * q : 128 * q + 128] for i in range(8)]
                xs = swap_vregs_rows(xs)
                for c in range(count):
                    result[start + c, pl.ds(pl.multiple_of(r * 8, 8), 8), lanes] = xs[c][
                        :, 0 : min(128, COLS - 128 * q)
                    ]
            return carry

        lax.fori_loop(0, ROWS // 8, turn_back, 0)
        span = pl.ds(start, count)
        copy = pltpu.make_async_copy(result.at[span], out_hbm.at[span], out_sem.at[half])
        copy.start()
        return copy

    add_group(0)
    add_group(1)
    halo_finish(coef_copies, coef, col_in.at[0], cor_in.at[0])

    def spread(i, carry):
        both = coef[i]
        ease = jnp.broadcast_to(both[0:1, :], (8, VC))
        east_b[i] = ease
        west_b[i] = pltpu.roll(ease, 1, 1)
        north_b[i] = jnp.broadcast_to(both[1:2, :], (8, VC))
        return carry

    lax.fori_loop(0, VR, spread, 0)

    add_group(2)
    add_group(3)
    halo_a = assemble(0, grid_a)
    halo_b = assemble(1, grid_b)
    out_a = smooth(0, halo_a, grid_a)
    out_b = smooth(1, halo_b, grid_b)

    everything = stage.at[pl.ds(1, DEV - 1)]
    pltpu.make_async_copy(everything, everything, send_sem).wait()
    out_a.wait()
    out_b.wait()


def on_device(
    adjoint_flux,
    ocean_wet,
    intersection_weight,
    pair_owner,
    pair_block,
    land_sea,
    east_coef,
    north_coef,
):
    vmem = pltpu.VMEM
    dma = pltpu.SemaphoreType.DMA
    return pl.pallas_call(
        kernel,
        out_shape=jax.ShapeDtypeStruct((2 * FIELDS, ROWS, COLS), F32),
        in_specs=[pl.BlockSpec(memory_space=pl.ANY)] * 8,
        out_specs=pl.BlockSpec(memory_space=pl.ANY),
        scratch_shapes=[
            vmem((HOURS, FIELDS, OB * BLK), BF16),
            vmem((OB, BLK), jnp.int32),
            vmem((OB, 2, BLK, BLK), BF16),
            vmem((2, OB), jnp.int32),
            vmem((2, OB), jnp.int32),
            vmem((ROWS, COLS), jnp.int32),
            vmem((ROWS, COLS), F32),
            vmem((ROWS, COLS), F32),
            vmem((2, 2 * OB + 1, 8, BLK), F32),
            vmem((8, DEV), jnp.int32),
            pltpu.SMEM((8, DEV), jnp.int32),
            vmem((DEV, DEV), F32),
            vmem((DEV, CAP * CH + 1, BLK), F32),
            vmem((DEV, CAP * CH + 1, BLK), F32),
            vmem((CH, 4 * WIDE, 128), F32),
            vmem((3, ROWS, VC), F32),
            vmem((VR, 8, VC), F32),
            vmem((VR, 8, VC), F32),
            vmem((VR, 8, VC), F32),
            vmem((VR, 8, VC), F32),
            vmem((VR, 8, VC), F32),
            vmem((VR, 8, VC), F32),
            vmem((VR, 8, VC), F32),
            vmem((2 * FIELDS, ROWS, COLS), F32),
            vmem((3, 2, 8, 128), F32),
            vmem((3, 2, 8, 128), F32),
            vmem((3, 2, 8, 128), F32),
            dma((6,)),
            dma((W_CHUNKS,)),
            dma((F_CHUNKS,)),
            dma,
            dma,
            dma((GROUPS,)),
            dma((3, 5)),
            dma((3, 5)),
            dma((2,)),
        ],
        compiler_params=pltpu.CompilerParams(
            collective_id=0, has_side_effects=True, vmem_limit_bytes=60 * 2**20
        ),
        cost_estimate=pl.CostEstimate(
            flops=4 * 10**8, bytes_accessed=12 * 10**6, transcendentals=0
        ),
    )(
        adjoint_flux,
        ocean_wet.reshape(OB, BLK),
        intersection_weight,
        pair_owner.T,
        pair_block.T,
        land_sea,
        east_coef,
        north_coef,
    )


def solution(mesh):
    in_specs = (
        P(None, None, ("tile", "sub")),
        P(("tile", "sub")),
        P(("tile", "sub"), None, None, None),
        P(("tile", "sub"), None),
        P(("tile", "sub"), None),
        P("tile", "sub"),
        P("tile", "sub"),
        P("tile", "sub"),
    )
    out_specs = P(None, "tile", "sub")
    return jax.shard_map(
        on_device, mesh=mesh, in_specs=in_specs, out_specs=out_specs, check_vma=False
    )
```

```python
import functools

import jax
import jax.numpy as jnp
import numpy as np
from jax import lax
from jax.experimental import pallas as pl
from jax.experimental.pallas import tpu as pltpu
from jax.sharding import PartitionSpec as P

PASSES = 4
HALO = 4
CAP = 4
GROUPS = 4
EACH = 32
HOURS = 6
FIELDS = 7
CH = 14
PARTS = ((0, 8), (8, 6))
BLK = 128
OB = 128
ROWS = 32
COLS = 720
ACROSS = 45
WIDE = 48
VR = ROWS + 8
VC = 768
DEV = 128
STRIDE = 37
W_CHUNKS = 8
F_CHUNKS = 8
MESH = pl.DeviceIdType.MESH
F32 = jnp.float32
BF16 = jnp.bfloat16


def iota(shape, dim):
    return lax.broadcasted_iota(jnp.int32, shape, dim)


def peer_of(tile, sub, j):
    o = (j * STRIDE) % DEV
    x = (tile // 16 + o // 32) % 4
    y = ((tile // 4) % 4 + (o // 8) % 4) % 4
    z = (sub * 2 + (tile // 2) % 2 + (o // 2) % 4) % 4
    c = (tile % 2 + o % 2) % 2
    return ((x * 4 + y) * 2 + z % 2) * 2 + c, z // 2


def swap_vregs_rows(xs):
    s = iota((8, 128), 0)
    xs = list(xs)
    for m in (1, 2, 4):
        low = (s // m) % 2 == 0
        for a in range(8):
            if (a // m) % 2 == 0:
                p, q = xs[a], xs[a + m]
                xs[a] = jnp.where(low, p, pltpu.roll(q, m, 0))
                xs[a + m] = jnp.where(low, pltpu.roll(p, 8 - m, 0), q)
    return xs


def swap_vregs_lanes(xs):
    g = iota((8, 128), 1) // 16
    xs = list(xs)
    for m in (1, 2, 4):
        low = (g // m) % 2 == 0
        for a in range(8):
            if (a // m) % 2 == 0:
                p, q = xs[a], xs[a + m]
                xs[a] = jnp.where(low, p, pltpu.roll(q, 16 * m, 1))
                xs[a + m] = jnp.where(low, pltpu.roll(p, 128 - 16 * m, 1), q)
    return xs


def gather_edges(v, col_out):
    lane = iota((8, 128), 1)
    for n in range(2):
        edge = jnp.zeros((8, 128), F32)
        for i in range(16):
            row = HALO + 16 * n + i
            left, right = v[row, :, 0:128], v[row, :, 640:768]
            if i:
                left = pltpu.roll(left, 8 * i, 1)
            right = pltpu.roll(right, (8 * i + 4 - 76) % 128, 1)
            edge = jnp.where((lane >= 8 * i) & (lane < 8 * i + 4), left, edge)
            edge = jnp.where((lane >= 8 * i + 4) & (lane < 8 * i + 8), right, edge)
        col_out[n] = edge


def halo_start(v, ready, tile, sub, col_out, col_in, cor_in, send, recv):
    up, down, other = (tile + 1) % 64, (tile + 63) % 64, 1 - sub
    parts = (
        (v.at[pl.ds(ROWS, HALO)], v.at[pl.ds(0, HALO)], (up, sub)),
        (v.at[pl.ds(HALO, HALO)], v.at[pl.ds(HALO + ROWS, HALO)], (down, sub)),
        (col_out, col_in, (tile, other)),
        (col_out.at[1], cor_in.at[0], (up, other)),
        (col_out.at[0], cor_in.at[1], (down, other)),
    )
    copies = []
    for i, (src, dst, to) in enumerate(parts):
        if i == 2 and not ready:
            gather_edges(v, col_out)
        copy = pltpu.make_async_remote_copy(
            src_ref=src,
            dst_ref=dst,
            send_sem=send.at[i],
            recv_sem=recv.at[i],
            device_id=to,
            device_id_type=MESH,
        )
        copy.start()
        copies.append(copy)
    return copies


def halo_finish(copies, v, col_in, cor_in):
    for copy in copies:
        copy.wait()
    lane = iota((8, 128), 1)
    for row in range(VR):
        i = row - HALO
        if i < 0:
            edge, off = cor_in[0], 8 * ((ROWS + i) % 16)
        elif i >= ROWS:
            edge, off = cor_in[1], 8 * (i - ROWS)
        else:
            edge, off = col_in[i // 16], 8 * (i % 16)
        own = v[row, :, 640:768]
        after = pltpu.roll(edge, (80 - off) % 128, 1)
        before = pltpu.roll(edge, (120 - off) % 128, 1)
        own = jnp.where((lane >= 80) & (lane < 84), after, jnp.where(lane >= 124, before, own))
        v[row, :, 640:768] = own


def kernel(
    flux_hbm,
    wet_hbm,
    w_hbm,
    owner_hbm,
    block_hbm,
    land_hbm,
    east_hbm,
    north_hbm,
    out,
    flux,
    wet,
    w,
    owner,
    block,
    land,
    east,
    north,
    items,
    index_v,
    index_s,
    labels,
    stage,
    recv,
    sums,
    padded,
    grid_a,
    grid_b,
    coef,
    east_b,
    west_b,
    north_b,
    spare,
    col_out,
    col_in,
    cor_in,
    in_sem,
    w_sem,
    f_sem,
    idx_sem,
    send_sem,
    recv_sem,
    halo_send,
    halo_recv,
):
    tile, sub = lax.axis_index("tile"), lax.axis_index("sub")
    me = tile * 2 + sub

    small = []
    for i, (src, dst) in enumerate(
        (
            (owner_hbm, owner),
            (block_hbm, block),
            (wet_hbm, wet),
            (land_hbm, land),
            (east_hbm, east),
            (north_hbm, north),
        )
    ):
        copy = pltpu.make_async_copy(src, dst, in_sem.at[i])
        copy.start()
        small.append(copy)
    blocks = OB // W_CHUNKS
    cells = blocks * BLK

    def bring(i):
        at = pl.ds(pl.multiple_of(i * cells, cells), cells)
        ocean = pl.ds(i * blocks, blocks)
        return (
            pltpu.make_async_copy(flux_hbm.at[:, :, at], flux.at[:, :, at], f_sem.at[i]),
            pltpu.make_async_copy(w_hbm.at[ocean], w.at[ocean], w_sem.at[i]),
        )

    for i in range(W_CHUNKS):
        for copy in bring(i):
            copy.start()

    barrier = pltpu.get_barrier_semaphore()

    def greet(i, carry):
        d = (me + i) % DEV
        pl.semaphore_signal(barrier, 1, device_id=(d // 2, d % 2), device_id_type=MESH)
        return carry

    lax.fori_loop(1, DEV, greet, 0)

    small[0].wait()
    small[1].wait()
    own = owner[...]
    blk = block[...]
    drow = iota((DEV, OB), 0)
    earlier = (iota((OB, OB), 0) < iota((OB, OB), 1)).astype(BF16)
    hit = [own[k : k + 1, :] == drow for k in range(2)]
    ones = [h.astype(F32) for h in hit]
    rank = [jnp.dot(o.astype(BF16), earlier, preferred_element_type=F32) for o in ones]
    rank[1] = rank[1] + jnp.sum(ones[0], axis=1, keepdims=True)
    wide = blk + (WIDE - ACROSS) * (
        (blk >= ACROSS).astype(jnp.int32)
        + (blk >= 2 * ACROSS).astype(jnp.int32)
        + (blk >= 3 * ACROSS).astype(jnp.int32)
    )
    wide = (wide + 1).astype(F32)
    position = iota((1, OB), 1).astype(F32) * 2.0
    first = iota((8, OB), 0)
    facts = []
    for k in range(2):
        facts.append(
            jnp.where(
                first == 0,
                wide[k : k + 1, :],
                jnp.where(first == 1, position + float(k - 2 * OB), 0.0),
            ).astype(BF16)
        )
    found = []
    for r in range(CAP):
        total = jnp.zeros((8, DEV), F32)
        for k in range(2):
            mine = jnp.where(rank[k] == float(r), ones[k], 0.0).astype(BF16)
            total = total + lax.dot_general(
                facts[k], mine, (((1,), (1,)), ((), ())), preferred_element_type=F32
            )
        found.append(total)
    row8 = iota((8, DEV), 0)
    index = jnp.zeros((8, DEV), F32)
    names = jnp.zeros((8, DEV), F32)
    for r in range(CAP):
        index = jnp.where(row8 == r, found[r][1:2, :] + float(2 * OB), index)
        names = jnp.where(row8 == r, found[r][0:1, :] - 1.0, names)
    index_v[...] = jnp.clip(index.astype(jnp.int32), 0, 2 * OB)
    to_smem = pltpu.make_async_copy(index_v, index_s, idx_sem)
    to_smem.start()
    labels[...] = jnp.concatenate([names, jnp.zeros((DEV - 8, DEV), F32)], axis=0).T

    padded[:, :, 640:VC] = jnp.zeros((3, ROWS, 128), F32)
    small[4].wait()
    small[5].wait()
    padded[0, :, 0:COLS] = east[...]
    row_global = tile * ROWS + iota((ROWS, COLS), 0)
    padded[1, :, 0:COLS] = jnp.where(row_global < 64 * ROWS - 1, north[...], 0.0)
    top = iota((8, VC), 0) == 0

    def lay(r, carry):
        at = pl.ds(pl.multiple_of(r * 8, 8), 8)
        ease, norse = padded[0, at, :], padded[1, at, :]
        for i in range(8):
            coef[HALO + 8 * r + i] = jnp.where(top, ease[i : i + 1, :], norse[i : i + 1, :])
        return carry

    lax.fori_loop(0, ROWS // 8, lay, 0)

    gather_edges(coef, col_out.at[0])

    items[0, 2 * OB] = jnp.zeros((8, BLK), F32)
    items[1, 2 * OB] = jnp.zeros((8, BLK), F32)
    small[2].wait()
    frac = [np.float32(h) / np.float32(HOURS) for h in range(HOURS)]
    blank = jnp.zeros((1, BLK), F32)

    def timed(p):
        at = pl.ds(pl.multiple_of(p * BLK, BLK), BLK)
        early = late = None
        for h in range(HOURS):
            x = flux[h, :, at].astype(F32)
            early = x if h == 0 else early + (np.float32(1.0) - frac[h]) * x
            if h:
                late = frac[h] * x if h == 1 else late + frac[h] * x
        mask = wet[pl.ds(p, 1), :].astype(F32)
        return jnp.concatenate([early * mask, late * mask, blank, blank], axis=0).astype(BF16)

    nothing = jnp.zeros((16, BLK), BF16)

    def chunk(i, carry):
        for copy in bring(i):
            copy.wait()
        for g in range(0, blocks, 2):
            p = i * blocks + g
            left = jnp.concatenate(
                [
                    jnp.concatenate([timed(p), nothing], axis=1),
                    jnp.concatenate([nothing, timed(p + 1)], axis=1),
                ],
                axis=0,
            )
            right = jnp.concatenate(
                [jnp.concatenate([w[p + e, 0], w[p + e, 1]], axis=1) for e in range(2)], axis=0
            )
            made = jnp.dot(left, right, preferred_element_type=F32)
            for e in range(2):
                for k in range(2):
                    for half in range(2):
                        items[half, 2 * (p + e) + k] = made[
                            16 * e + 8 * half : 16 * e + 8 * half + 8, BLK * k : BLK * k + BLK
                        ]
        return carry

    lax.fori_loop(0, W_CHUNKS, chunk, 0)

    to_smem.wait()
    pl.semaphore_wait(barrier, DEV - 1)

    coef_copies = halo_start(
        coef, True, tile, sub, col_out.at[0], col_in.at[0], cor_in.at[0], halo_send.at[0], halo_recv.at[0]
    )

    def pack(d, into):
        for r in range(CAP):
            at = index_s[r, d]
            for half, (start, count) in enumerate(PARTS):
                row = r * CH + start
                into[row : row + count, :] = items[half, at][0:count, :]
        into[CAP * CH : CAP * CH + 1, :] = labels[pl.ds(d, 1), :]

    for g in range(GROUPS):

        def send(j, carry, g=g):
            t, u = peer_of(tile, sub, j)
            pack(t * 2 + u, stage.at[j])
            pltpu.make_async_remote_copy(
                src_ref=stage.at[j],
                dst_ref=recv.at[j],
                send_sem=send_sem,
                recv_sem=recv_sem.at[g],
                device_id=(t, u),
                device_id_type=MESH,
            ).start()
            return carry

        lax.fori_loop(max(1, EACH * g), EACH * (g + 1), send, 0)

    pack(me, recv.at[0])

    small[3].wait()
    padded[2, :, 0:COLS] = land[...].astype(F32)
    slot_rows = iota((4 * WIDE, CAP * EACH), 0).astype(F32)

    def add_group(g):
        low = max(1, EACH * g)
        everything = recv.at[pl.ds(low, EACH * (g + 1) - low)]
        pltpu.make_async_copy(everything, everything, recv_sem.at[g]).wait()
        here = slice(EACH * g, EACH * (g + 1))
        named = recv[here, CAP * CH, :].T
        line = jnp.concatenate([named[r : r + 1, :] for r in range(CAP)], axis=1)
        picked = (slot_rows == line).astype(BF16)
        for f in range(0, CH, 2):
            got = jnp.concatenate(
                [
                    jnp.concatenate(
                        [recv[here, r * CH + f + e, :].astype(BF16) for r in range(CAP)], axis=0
                    )
                    for e in range(2)
                ],
                axis=1,
            )
            both = jnp.dot(picked, got, preferred_element_type=F32)
            for e in range(2):
                part = both[:, 128 * e : 128 * e + 128]
                sums[f + e] = part if g == 0 else sums[f + e] + part

    def assemble(half, grid):
        start, count = PARTS[half]
        none = jnp.zeros((8, 128), F32)

        def place(r, carry):
            for q in range(6):
                lanes = slice(128 * q, 128 * q + 128)
                at = pl.ds(pl.multiple_of(r * WIDE + 8 * q, 8), 8)
                xs = [sums[start + f, at, :] if f < count else none for f in range(8)]
                xs = swap_vregs_lanes(swap_vregs_rows(xs))
                sea = padded[2, pl.ds(pl.multiple_of(r * 8, 8), 8), lanes]
                for i in range(8):
                    grid[HALO + 8 * r + i, :, lanes] = xs[i] * sea[i : i + 1, :]
            return carry

        lax.fori_loop(0, ROWS // 8, place, 0)
        return halo_start(
            grid,
            False,
            tile,
            sub,
            col_out.at[1 + half],
            col_in.at[1 + half],
            cor_in.at[1 + half],
            halo_send.at[1 + half],
            halo_recv.at[1 + half],
        )

    def smooth(half, copies, grid):
        start, count = PARTS[half]
        halo_finish(copies, grid, col_in.at[1 + half], cor_in.at[1 + half])
        def lines(src, dst, base, n):
            v = src[base]
            below = north_b[base - 1] * (v - src[base - 1])
            for k in range(n):
                at = base + k
                above = src[at + 1]
                rise = north_b[at] * (above - v)
                east_side = east_b[at] * (pltpu.roll(v, VC - 1, 1) - v)
                west_side = west_b[at] * (v - pltpu.roll(v, 1, 1))
                dst[at] = v + (east_side - west_side) + (rise - below)
                v, below = above, rise

        for turn in range(PASSES):
            src, dst = (grid, spare) if turn % 2 == 0 else (spare, grid)
            low, count_rows = turn + 1, VR - 2 - 2 * turn

            def block_of(n, carry, src=src, dst=dst, low=low):
                lines(src, dst, low + 8 * n, 8)
                return carry

            lax.fori_loop(0, count_rows // 8, block_of, 0)
            if count_rows % 8:
                lines(src, dst, low + count_rows // 8 * 8, count_rows % 8)

        def turn_back(r, carry):
            for q in range(6):
                lanes = slice(128 * q, min(128 * q + 128, COLS))
                xs = [grid[HALO + 8 * r + i, :, 128 * q : 128 * q + 128] for i in range(8)]
                xs = swap_vregs_rows(xs)
                for c in range(count):
                    out[start + c, pl.ds(pl.multiple_of(r * 8, 8), 8), lanes] = xs[c][
                        :, 0 : min(128, COLS - 128 * q)
                    ]
            return carry

        lax.fori_loop(0, ROWS // 8, turn_back, 0)

    add_group(0)
    add_group(1)
    halo_finish(coef_copies, coef, col_in.at[0], cor_in.at[0])

    def spread(i, carry):
        both = coef[i]
        ease = jnp.broadcast_to(both[0:1, :], (8, VC))
        east_b[i] = ease
        west_b[i] = pltpu.roll(ease, 1, 1)
        north_b[i] = jnp.broadcast_to(both[1:2, :], (8, VC))
        return carry

    lax.fori_loop(0, VR, spread, 0)

    add_group(2)
    add_group(3)
    halo_a = assemble(0, grid_a)
    halo_b = assemble(1, grid_b)
    smooth(0, halo_a, grid_a)
    smooth(1, halo_b, grid_b)

    everything = stage.at[pl.ds(1, DEV - 1)]
    pltpu.make_async_copy(everything, everything, send_sem).wait()


def on_device(
    adjoint_flux,
    ocean_wet,
    intersection_weight,
    pair_owner,
    pair_block,
    land_sea,
    east_coef,
    north_coef,
):
    vmem = pltpu.VMEM
    dma = pltpu.SemaphoreType.DMA
    return pl.pallas_call(
        kernel,
        out_shape=pltpu.VMEM((2 * FIELDS, ROWS, COLS), F32),
        in_specs=[pl.BlockSpec(memory_space=pl.ANY)] * 8,
        out_specs=pl.BlockSpec(memory_space=pltpu.VMEM),
        scratch_shapes=[
            vmem((HOURS, FIELDS, OB * BLK), BF16),
            vmem((OB, BLK), jnp.int32),
            vmem((OB, 2, BLK, BLK), BF16),
            vmem((2, OB), jnp.int32),
            vmem((2, OB), jnp.int32),
            vmem((ROWS, COLS), jnp.int32),
            vmem((ROWS, COLS), F32),
            vmem((ROWS, COLS), F32),
            vmem((2, 2 * OB + 1, 8, BLK), F32),
            vmem((8, DEV), jnp.int32),
            pltpu.SMEM((8, DEV), jnp.int32),
            vmem((DEV, DEV), F32),
            vmem((DEV, CAP * CH + 1, BLK), F32),
            vmem((DEV, CAP * CH + 1, BLK), F32),
            vmem((CH, 4 * WIDE, 128), F32),
            vmem((3, ROWS, VC), F32),
            vmem((VR, 8, VC), F32),
            vmem((VR, 8, VC), F32),
            vmem((VR, 8, VC), F32),
            vmem((VR, 8, VC), F32),
            vmem((VR, 8, VC), F32),
            vmem((VR, 8, VC), F32),
            vmem((VR, 8, VC), F32),
            vmem((3, 2, 8, 128), F32),
            vmem((3, 2, 8, 128), F32),
            vmem((3, 2, 8, 128), F32),
            dma((6,)),
            dma((W_CHUNKS,)),
            dma((F_CHUNKS,)),
            dma,
            dma,
            dma((GROUPS,)),
            dma((3, 5)),
            dma((3, 5)),
        ],
        compiler_params=pltpu.CompilerParams(
            collective_id=0, has_side_effects=True, vmem_limit_bytes=54 * 2**20
        ),
        cost_estimate=pl.CostEstimate(
            flops=4 * 10**8, bytes_accessed=12 * 10**6, transcendentals=0
        ),
    )(
        adjoint_flux,
        ocean_wet.reshape(OB, BLK),
        intersection_weight,
        pair_owner.T,
        pair_block.T,
        land_sea,
        east_coef,
        north_coef,
    )


def solution(mesh):
    in_specs = (
        P(None, None, ("tile", "sub")),
        P(("tile", "sub")),
        P(("tile", "sub"), None, None, None),
        P(("tile", "sub"), None),
        P(("tile", "sub"), None),
        P("tile", "sub"),
        P("tile", "sub"),
        P("tile", "sub"),
    )
    out_specs = P(None, "tile", "sub")
    return jax.shard_map(
        on_device, mesh=mesh, in_specs=in_specs, out_specs=out_specs, check_vma=False
    )
```

```python
import functools

import jax
import jax.numpy as jnp
import numpy as np
from jax import lax
from jax.experimental import pallas as pl
from jax.experimental.pallas import tpu as pltpu
from jax.sharding import PartitionSpec as P

PASSES = 4
HALO = 4
CAP = 4
GROUPS = 4
EACH = 32
HOURS = 6
FIELDS = 7
CH = 14
PARTS = ((0, 8), (8, 6))
BLK = 128
OB = 128
ROWS = 32
COLS = 720
ACROSS = 45
WIDE = 48
VR = ROWS + 8
VC = 768
DEV = 128
STRIDE = 53
W_CHUNKS = 8
F_CHUNKS = 8
MESH = pl.DeviceIdType.MESH
F32 = jnp.float32
BF16 = jnp.bfloat16


def iota(shape, dim):
    return lax.broadcasted_iota(jnp.int32, shape, dim)


def peer_of(tile, sub, j):
    o = (j * STRIDE) % DEV
    x = (tile // 16 + o // 32) % 4
    y = ((tile // 4) % 4 + (o // 8) % 4) % 4
    z = (sub * 2 + (tile // 2) % 2 + (o // 2) % 4) % 4
    c = (tile % 2 + o % 2) % 2
    return ((x * 4 + y) * 2 + z % 2) * 2 + c, z // 2


def swap_vregs_rows(xs):
    s = iota((8, 128), 0)
    xs = list(xs)
    for m in (1, 2, 4):
        low = (s // m) % 2 == 0
        for a in range(8):
            if (a // m) % 2 == 0:
                p, q = xs[a], xs[a + m]
                xs[a] = jnp.where(low, p, pltpu.roll(q, m, 0))
                xs[a + m] = jnp.where(low, pltpu.roll(p, 8 - m, 0), q)
    return xs


def swap_vregs_lanes(xs):
    g = iota((8, 128), 1) // 16
    xs = list(xs)
    for m in (1, 2, 4):
        low = (g // m) % 2 == 0
        for a in range(8):
            if (a // m) % 2 == 0:
                p, q = xs[a], xs[a + m]
                xs[a] = jnp.where(low, p, pltpu.roll(q, 16 * m, 1))
                xs[a + m] = jnp.where(low, pltpu.roll(p, 128 - 16 * m, 1), q)
    return xs


def gather_edges(v, col_out):
    lane = iota((8, 128), 1)
    for n in range(2):
        edge = jnp.zeros((8, 128), F32)
        for i in range(16):
            row = HALO + 16 * n + i
            left, right = v[row, :, 0:128], v[row, :, 640:768]
            if i:
                left = pltpu.roll(left, 8 * i, 1)
            right = pltpu.roll(right, (8 * i + 4 - 76) % 128, 1)
            edge = jnp.where((lane >= 8 * i) & (lane < 8 * i + 4), left, edge)
            edge = jnp.where((lane >= 8 * i + 4) & (lane < 8 * i + 8), right, edge)
        col_out[n] = edge


def halo_start(v, ready, tile, sub, col_out, col_in, cor_in, send, recv):
    up, down, other = (tile + 1) % 64, (tile + 63) % 64, 1 - sub
    parts = (
        (v.at[pl.ds(ROWS, HALO)], v.at[pl.ds(0, HALO)], (up, sub)),
        (v.at[pl.ds(HALO, HALO)], v.at[pl.ds(HALO + ROWS, HALO)], (down, sub)),
        (col_out, col_in, (tile, other)),
        (col_out.at[1], cor_in.at[0], (up, other)),
        (col_out.at[0], cor_in.at[1], (down, other)),
    )
    copies = []
    for i, (src, dst, to) in enumerate(parts):
        if i == 2 and not ready:
            gather_edges(v, col_out)
        copy = pltpu.make_async_remote_copy(
            src_ref=src,
            dst_ref=dst,
            send_sem=send.at[i],
            recv_sem=recv.at[i],
            device_id=to,
            device_id_type=MESH,
        )
        copy.start()
        copies.append(copy)
    return copies


def halo_finish(copies, v, col_in, cor_in):
    for copy in copies:
        copy.wait()
    lane = iota((8, 128), 1)
    for row in range(VR):
        i = row - HALO
        if i < 0:
            edge, off = cor_in[0], 8 * ((ROWS + i) % 16)
        elif i >= ROWS:
            edge, off = cor_in[1], 8 * (i - ROWS)
        else:
            edge, off = col_in[i // 16], 8 * (i % 16)
        own = v[row, :, 640:768]
        after = pltpu.roll(edge, (80 - off) % 128, 1)
        before = pltpu.roll(edge, (120 - off) % 128, 1)
        own = jnp.where((lane >= 80) & (lane < 84), after, jnp.where(lane >= 124, before, own))
        v[row, :, 640:768] = own


def kernel(
    flux_hbm,
    wet_hbm,
    w_hbm,
    owner_hbm,
    block_hbm,
    land_hbm,
    east_hbm,
    north_hbm,
    out,
    flux,
    wet,
    w,
    owner,
    block,
    land,
    east,
    north,
    items,
    index_v,
    index_s,
    labels,
    stage,
    recv,
    sums,
    padded,
    grid_a,
    grid_b,
    coef,
    east_b,
    west_b,
    north_b,
    spare,
    col_out,
    col_in,
    cor_in,
    in_sem,
    w_sem,
    f_sem,
    idx_sem,
    send_sem,
    recv_sem,
    halo_send,
    halo_recv,
):
    tile, sub = lax.axis_index("tile"), lax.axis_index("sub")
    me = tile * 2 + sub

    small = []
    for i, (src, dst) in enumerate(
        (
            (owner_hbm, owner),
            (block_hbm, block),
            (wet_hbm, wet),
            (land_hbm, land),
            (east_hbm, east),
            (north_hbm, north),
        )
    ):
        copy = pltpu.make_async_copy(src, dst, in_sem.at[i])
        copy.start()
        small.append(copy)
    blocks = OB // W_CHUNKS
    cells = blocks * BLK

    def bring(i):
        at = pl.ds(pl.multiple_of(i * cells, cells), cells)
        ocean = pl.ds(i * blocks, blocks)
        return (
            pltpu.make_async_copy(flux_hbm.at[:, :, at], flux.at[:, :, at], f_sem.at[i]),
            pltpu.make_async_copy(w_hbm.at[ocean], w.at[ocean], w_sem.at[i]),
        )

    for i in range(W_CHUNKS):
        for copy in bring(i):
            copy.start()

    barrier = pltpu.get_barrier_semaphore()

    def greet(i, carry):
        d = (me + i) % DEV
        pl.semaphore_signal(barrier, 1, device_id=(d // 2, d % 2), device_id_type=MESH)
        return carry

    lax.fori_loop(1, DEV, greet, 0)

    small[0].wait()
    small[1].wait()
    own = owner[...]
    blk = block[...]
    drow = iota((DEV, OB), 0)
    earlier = (iota((OB, OB), 0) < iota((OB, OB), 1)).astype(BF16)
    hit = [own[k : k + 1, :] == drow for k in range(2)]
    ones = [h.astype(F32) for h in hit]
    rank = [jnp.dot(o.astype(BF16), earlier, preferred_element_type=F32) for o in ones]
    rank[1] = rank[1] + jnp.sum(ones[0], axis=1, keepdims=True)
    wide = blk + (WIDE - ACROSS) * (
        (blk >= ACROSS).astype(jnp.int32)
        + (blk >= 2 * ACROSS).astype(jnp.int32)
        + (blk >= 3 * ACROSS).astype(jnp.int32)
    )
    wide = (wide + 1).astype(F32)
    position = iota((1, OB), 1).astype(F32) * 2.0
    first = iota((8, OB), 0)
    facts = []
    for k in range(2):
        facts.append(
            jnp.where(
                first == 0,
                wide[k : k + 1, :],
                jnp.where(first == 1, position + float(k - 2 * OB), 0.0),
            ).astype(BF16)
        )
    found = []
    for r in range(CAP):
        total = jnp.zeros((8, DEV), F32)
        for k in range(2):
            mine = jnp.where(rank[k] == float(r), ones[k], 0.0).astype(BF16)
            total = total + lax.dot_general(
                facts[k], mine, (((1,), (1,)), ((), ())), preferred_element_type=F32
            )
        found.append(total)
    row8 = iota((8, DEV), 0)
    index = jnp.zeros((8, DEV), F32)
    names = jnp.zeros((8, DEV), F32)
    for r in range(CAP):
        index = jnp.where(row8 == r, found[r][1:2, :] + float(2 * OB), index)
        names = jnp.where(row8 == r, found[r][0:1, :] - 1.0, names)
    index_v[...] = jnp.clip(index.astype(jnp.int32), 0, 2 * OB)
    to_smem = pltpu.make_async_copy(index_v, index_s, idx_sem)
    to_smem.start()
    labels[...] = jnp.concatenate([names, jnp.zeros((DEV - 8, DEV), F32)], axis=0).T

    padded[:, :, 640:VC] = jnp.zeros((3, ROWS, 128), F32)
    small[4].wait()
    small[5].wait()
    padded[0, :, 0:COLS] = east[...]
    row_global = tile * ROWS + iota((ROWS, COLS), 0)
    padded[1, :, 0:COLS] = jnp.where(row_global < 64 * ROWS - 1, north[...], 0.0)
    top = iota((8, VC), 0) == 0

    def lay(r, carry):
        at = pl.ds(pl.multiple_of(r * 8, 8), 8)
        ease, norse = padded[0, at, :], padded[1, at, :]
        for i in range(8):
            coef[HALO + 8 * r + i] = jnp.where(top, ease[i : i + 1, :], norse[i : i + 1, :])
        return carry

    lax.fori_loop(0, ROWS // 8, lay, 0)

    gather_edges(coef, col_out.at[0])

    items[0, 2 * OB] = jnp.zeros((8, BLK), F32)
    items[1, 2 * OB] = jnp.zeros((8, BLK), F32)
    small[2].wait()
    frac = [np.float32(h) / np.float32(HOURS) for h in range(HOURS)]
    blank = jnp.zeros((1, BLK), F32)

    def timed(p):
        at = pl.ds(pl.multiple_of(p * BLK, BLK), BLK)
        early = late = None
        for h in range(HOURS):
            x = flux[h, :, at].astype(F32)
            early = x if h == 0 else early + (np.float32(1.0) - frac[h]) * x
            if h:
                late = frac[h] * x if h == 1 else late + frac[h] * x
        mask = wet[pl.ds(p, 1), :].astype(F32)
        return jnp.concatenate([early * mask, late * mask, blank, blank], axis=0).astype(BF16)

    nothing = jnp.zeros((16, BLK), BF16)

    def chunk(i, carry):
        for copy in bring(i):
            copy.wait()
        for g in range(0, blocks, 2):
            p = i * blocks + g
            left = jnp.concatenate(
                [
                    jnp.concatenate([timed(p), nothing], axis=1),
                    jnp.concatenate([nothing, timed(p + 1)], axis=1),
                ],
                axis=0,
            )
            right = jnp.concatenate(
                [jnp.concatenate([w[p + e, 0], w[p + e, 1]], axis=1) for e in range(2)], axis=0
            )
            made = jnp.dot(left, right, preferred_element_type=F32)
            for e in range(2):
                for k in range(2):
                    for half in range(2):
                        items[half, 2 * (p + e) + k] = made[
                            16 * e + 8 * half : 16 * e + 8 * half + 8, BLK * k : BLK * k + BLK
                        ]
        return carry

    lax.fori_loop(0, W_CHUNKS, chunk, 0)

    to_smem.wait()
    pl.semaphore_wait(barrier, DEV - 1)

    coef_copies = halo_start(
        coef, True, tile, sub, col_out.at[0], col_in.at[0], cor_in.at[0], halo_send.at[0], halo_recv.at[0]
    )

    def pack(d, into):
        for r in range(CAP):
            at = index_s[r, d]
            for half, (start, count) in enumerate(PARTS):
                row = r * CH + start
                into[row : row + count, :] = items[half, at][0:count, :]
        into[CAP * CH : CAP * CH + 1, :] = labels[pl.ds(d, 1), :]

    for g in range(GROUPS):

        def send(j, carry, g=g):
            t, u = peer_of(tile, sub, j)
            pack(t * 2 + u, stage.at[j])
            pltpu.make_async_remote_copy(
                src_ref=stage.at[j],
                dst_ref=recv.at[j],
                send_sem=send_sem,
                recv_sem=recv_sem.at[g],
                device_id=(t, u),
                device_id_type=MESH,
            ).start()
            return carry

        lax.fori_loop(max(1, EACH * g), EACH * (g + 1), send, 0)

    pack(me, recv.at[0])

    small[3].wait()
    padded[2, :, 0:COLS] = land[...].astype(F32)
    slot_rows = iota((4 * WIDE, CAP * EACH), 0).astype(F32)

    def arrive(g):
        low = max(1, EACH * g)
        everything = recv.at[pl.ds(low, EACH * (g + 1) - low)]
        pltpu.make_async_copy(everything, everything, recv_sem.at[g]).wait()
        here = slice(EACH * g, EACH * (g + 1))
        named = recv[here, CAP * CH, :].T
        line = jnp.concatenate([named[r : r + 1, :] for r in range(CAP)], axis=1)
        return (slot_rows == line).astype(BF16)

    def add_group(g, picked, first, last):
        here = slice(EACH * g, EACH * (g + 1))
        for f in range(first, last, 2):
            got = jnp.concatenate(
                [
                    jnp.concatenate(
                        [recv[here, r * CH + f + e, :].astype(BF16) for r in range(CAP)], axis=0
                    )
                    for e in range(2)
                ],
                axis=1,
            )
            both = jnp.dot(picked, got, preferred_element_type=F32)
            for e in range(2):
                part = both[:, 128 * e : 128 * e + 128]
                sums[f + e] = part if g == 0 else sums[f + e] + part

    def assemble(half, grid):
        start, count = PARTS[half]
        none = jnp.zeros((8, 128), F32)

        def place(r, carry):
            for q in range(6):
                lanes = slice(128 * q, 128 * q + 128)
                at = pl.ds(pl.multiple_of(r * WIDE + 8 * q, 8), 8)
                xs = [sums[start + f, at, :] if f < count else none for f in range(8)]
                xs = swap_vregs_lanes(swap_vregs_rows(xs))
                sea = padded[2, pl.ds(pl.multiple_of(r * 8, 8), 8), lanes]
                for i in range(8):
                    grid[HALO + 8 * r + i, :, lanes] = xs[i] * sea[i : i + 1, :]
            return carry

        lax.fori_loop(0, ROWS // 8, place, 0)
        return halo_start(
            grid,
            False,
            tile,
            sub,
            col_out.at[1 + half],
            col_in.at[1 + half],
            cor_in.at[1 + half],
            halo_send.at[1 + half],
            halo_recv.at[1 + half],
        )

    def smooth(half, copies, grid):
        start, count = PARTS[half]
        halo_finish(copies, grid, col_in.at[1 + half], cor_in.at[1 + half])
        def lines(src, dst, base, n):
            v = src[base]
            below = north_b[base - 1] * (v - src[base - 1])
            for k in range(n):
                at = base + k
                above = src[at + 1]
                rise = north_b[at] * (above - v)
                east_side = east_b[at] * (pltpu.roll(v, VC - 1, 1) - v)
                west_side = west_b[at] * (v - pltpu.roll(v, 1, 1))
                dst[at] = v + (east_side - west_side) + (rise - below)
                v, below = above, rise

        for turn in range(PASSES):
            src, dst = (grid, spare) if turn % 2 == 0 else (spare, grid)
            low, count_rows = turn + 1, VR - 2 - 2 * turn

            def block_of(n, carry, src=src, dst=dst, low=low):
                lines(src, dst, low + 8 * n, 8)
                return carry

            lax.fori_loop(0, count_rows // 8, block_of, 0)
            if count_rows % 8:
                lines(src, dst, low + count_rows // 8 * 8, count_rows % 8)

        def turn_back(r, carry):
            for q in range(6):
                lanes = slice(128 * q, min(128 * q + 128, COLS))
                xs = [grid[HALO + 8 * r + i, :, 128 * q : 128 * q + 128] for i in range(8)]
                xs = swap_vregs_rows(xs)
                for c in range(count):
                    out[start + c, pl.ds(pl.multiple_of(r * 8, 8), 8), lanes] = xs[c][
                        :, 0 : min(128, COLS - 128 * q)
                    ]
            return carry

        lax.fori_loop(0, ROWS // 8, turn_back, 0)

    for g in range(GROUPS // 2):
        add_group(g, arrive(g), 0, CH)
    for g in range(GROUPS // 2, GROUPS - 1):
        add_group(g, arrive(g), 0, CH)
    final = arrive(GROUPS - 1)
    halves = []
    for half, grid in ((0, grid_a), (1, grid_b)):
        start, count = PARTS[half]
        add_group(GROUPS - 1, final, start, start + count)
        halves.append(assemble(half, grid))
    halo_finish(coef_copies, coef, col_in.at[0], cor_in.at[0])

    def spread(i, carry):
        both = coef[i]
        ease = jnp.broadcast_to(both[0:1, :], (8, VC))
        east_b[i] = ease
        west_b[i] = pltpu.roll(ease, 1, 1)
        north_b[i] = jnp.broadcast_to(both[1:2, :], (8, VC))
        return carry

    lax.fori_loop(0, VR, spread, 0)

    smooth(0, halves[0], grid_a)
    smooth(1, halves[1], grid_b)

    everything = stage.at[pl.ds(1, DEV - 1)]
    pltpu.make_async_copy(everything, everything, send_sem).wait()


def on_device(
    adjoint_flux,
    ocean_wet,
    intersection_weight,
    pair_owner,
    pair_block,
    land_sea,
    east_coef,
    north_coef,
):
    vmem = pltpu.VMEM
    dma = pltpu.SemaphoreType.DMA
    return pl.pallas_call(
        kernel,
        out_shape=pltpu.VMEM((2 * FIELDS, ROWS, COLS), F32),
        in_specs=[pl.BlockSpec(memory_space=pl.ANY)] * 8,
        out_specs=pl.BlockSpec(memory_space=pltpu.VMEM),
        scratch_shapes=[
            vmem((HOURS, FIELDS, OB * BLK), BF16),
            vmem((OB, BLK), jnp.int32),
            vmem((OB, 2, BLK, BLK), BF16),
            vmem((2, OB), jnp.int32),
            vmem((2, OB), jnp.int32),
            vmem((ROWS, COLS), jnp.int32),
            vmem((ROWS, COLS), F32),
            vmem((ROWS, COLS), F32),
            vmem((2, 2 * OB + 1, 8, BLK), F32),
            vmem((8, DEV), jnp.int32),
            pltpu.SMEM((8, DEV), jnp.int32),
            vmem((DEV, DEV), F32),
            vmem((DEV, CAP * CH + 1, BLK), F32),
            vmem((DEV, CAP * CH + 1, BLK), F32),
            vmem((CH, 4 * WIDE, 128), F32),
            vmem((3, ROWS, VC), F32),
            vmem((VR, 8, VC), F32),
            vmem((VR, 8, VC), F32),
            vmem((VR, 8, VC), F32),
            vmem((VR, 8, VC), F32),
            vmem((VR, 8, VC), F32),
            vmem((VR, 8, VC), F32),
            vmem((VR, 8, VC), F32),
            vmem((3, 2, 8, 128), F32),
            vmem((3, 2, 8, 128), F32),
            vmem((3, 2, 8, 128), F32),
            dma((6,)),
            dma((W_CHUNKS,)),
            dma((F_CHUNKS,)),
            dma,
            dma,
            dma((GROUPS,)),
            dma((3, 5)),
            dma((3, 5)),
        ],
        compiler_params=pltpu.CompilerParams(
            collective_id=0, has_side_effects=True, vmem_limit_bytes=54 * 2**20
        ),
        cost_estimate=pl.CostEstimate(
            flops=4 * 10**8, bytes_accessed=12 * 10**6, transcendentals=0
        ),
    )(
        adjoint_flux,
        ocean_wet.reshape(OB, BLK),
        intersection_weight,
        pair_owner.T,
        pair_block.T,
        land_sea,
        east_coef,
        north_coef,
    )


def solution(mesh):
    in_specs = (
        P(None, None, ("tile", "sub")),
        P(("tile", "sub")),
        P(("tile", "sub"), None, None, None),
        P(("tile", "sub"), None),
        P(("tile", "sub"), None),
        P("tile", "sub"),
        P("tile", "sub"),
        P("tile", "sub"),
    )
    out_specs = P(None, "tile", "sub")
    return jax.shard_map(
        on_device, mesh=mesh, in_specs=in_specs, out_specs=out_specs, check_vma=False
    )
```

```python
import functools

import jax
import jax.numpy as jnp
import numpy as np
from jax import lax
from jax.experimental import pallas as pl
from jax.experimental.pallas import tpu as pltpu
from jax.sharding import PartitionSpec as P

PASSES = 4
HALO = 4
CAP = 4
GROUPS = 4
EACH = 32
HOURS = 6
FIELDS = 7
CH = 14
PARTS = ((0, 8), (8, 6))
BLK = 128
OB = 128
ROWS = 32
COLS = 720
ACROSS = 45
WIDE = 48
VR = ROWS + 8
VC = 768
DEV = 128
STRIDE = 53
W_CHUNKS = 8
F_CHUNKS = 8
MESH = pl.DeviceIdType.MESH
F32 = jnp.float32
BF16 = jnp.bfloat16


def iota(shape, dim):
    return lax.broadcasted_iota(jnp.int32, shape, dim)


def peer_of(tile, sub, j):
    o = (j * STRIDE) % DEV
    x = (tile // 16 + o // 32) % 4
    y = ((tile // 4) % 4 + (o // 8) % 4) % 4
    z = (sub * 2 + (tile // 2) % 2 + (o // 2) % 4) % 4
    c = (tile % 2 + o % 2) % 2
    return ((x * 4 + y) * 2 + z % 2) * 2 + c, z // 2


def swap_vregs_rows(xs):
    s = iota((8, 128), 0)
    xs = list(xs)
    for m in (1, 2, 4):
        low = (s // m) % 2 == 0
        for a in range(8):
            if (a // m) % 2 == 0:
                p, q = xs[a], xs[a + m]
                xs[a] = jnp.where(low, p, pltpu.roll(q, m, 0))
                xs[a + m] = jnp.where(low, pltpu.roll(p, 8 - m, 0), q)
    return xs


def swap_vregs_lanes(xs):
    g = iota((8, 128), 1) // 16
    xs = list(xs)
    for m in (1, 2, 4):
        low = (g // m) % 2 == 0
        for a in range(8):
            if (a // m) % 2 == 0:
                p, q = xs[a], xs[a + m]
                xs[a] = jnp.where(low, p, pltpu.roll(q, 16 * m, 1))
                xs[a + m] = jnp.where(low, pltpu.roll(p, 128 - 16 * m, 1), q)
    return xs


def gather_edges(v, col_out):
    lane = iota((8, 128), 1)
    for n in range(2):
        edge = jnp.zeros((8, 128), F32)
        for i in range(16):
            row = HALO + 16 * n + i
            left, right = v[row, :, 0:128], v[row, :, 640:768]
            if i:
                left = pltpu.roll(left, 8 * i, 1)
            right = pltpu.roll(right, (8 * i + 4 - 76) % 128, 1)
            edge = jnp.where((lane >= 8 * i) & (lane < 8 * i + 4), left, edge)
            edge = jnp.where((lane >= 8 * i + 4) & (lane < 8 * i + 8), right, edge)
        col_out[n] = edge


def halo_start(v, ready, tile, sub, col_out, col_in, cor_in, send, recv):
    up, down, other = (tile + 1) % 64, (tile + 63) % 64, 1 - sub
    parts = (
        (v.at[pl.ds(ROWS, HALO)], v.at[pl.ds(0, HALO)], (up, sub)),
        (v.at[pl.ds(HALO, HALO)], v.at[pl.ds(HALO + ROWS, HALO)], (down, sub)),
        (col_out, col_in, (tile, other)),
        (col_out.at[1], cor_in.at[0], (up, other)),
        (col_out.at[0], cor_in.at[1], (down, other)),
    )
    copies = []
    for i, (src, dst, to) in enumerate(parts):
        if i == 2 and not ready:
            gather_edges(v, col_out)
        copy = pltpu.make_async_remote_copy(
            src_ref=src,
            dst_ref=dst,
            send_sem=send.at[i],
            recv_sem=recv.at[i],
            device_id=to,
            device_id_type=MESH,
        )
        copy.start()
        copies.append(copy)
    return copies


def halo_finish(copies, v, col_in, cor_in):
    for copy in copies:
        copy.wait()
    lane = iota((8, 128), 1)
    for row in range(VR):
        i = row - HALO
        if i < 0:
            edge, off = cor_in[0], 8 * ((ROWS + i) % 16)
        elif i >= ROWS:
            edge, off = cor_in[1], 8 * (i - ROWS)
        else:
            edge, off = col_in[i // 16], 8 * (i % 16)
        own = v[row, :, 640:768]
        after = pltpu.roll(edge, (80 - off) % 128, 1)
        before = pltpu.roll(edge, (120 - off) % 128, 1)
        own = jnp.where((lane >= 80) & (lane < 84), after, jnp.where(lane >= 124, before, own))
        v[row, :, 640:768] = own


def kernel(
    flux_hbm,
    wet_hbm,
    w_hbm,
    owner_hbm,
    block_hbm,
    land_hbm,
    east_hbm,
    north_hbm,
    out,
    flux,
    wet,
    w,
    owner,
    block,
    land,
    east,
    north,
    items,
    index_v,
    index_s,
    labels,
    stage,
    recv,
    sums,
    padded,
    grid_a,
    grid_b,
    coef,
    east_b,
    west_b,
    north_b,
    spare,
    col_out,
    col_in,
    cor_in,
    in_sem,
    w_sem,
    f_sem,
    idx_sem,
    send_sem,
    recv_sem,
    halo_send,
    halo_recv,
):
    tile, sub = lax.axis_index("tile"), lax.axis_index("sub")
    me = tile * 2 + sub

    small = []
    for i, (src, dst) in enumerate(
        (
            (owner_hbm, owner),
            (block_hbm, block),
            (wet_hbm, wet),
            (land_hbm, land),
            (east_hbm, east),
            (north_hbm, north),
        )
    ):
        copy = pltpu.make_async_copy(src, dst, in_sem.at[i])
        copy.start()
        small.append(copy)
    blocks = OB // W_CHUNKS
    cells = blocks * BLK

    def bring(i):
        at = pl.ds(pl.multiple_of(i * cells, cells), cells)
        ocean = pl.ds(i * blocks, blocks)
        return (
            pltpu.make_async_copy(flux_hbm.at[:, :, at], flux.at[:, :, at], f_sem.at[i]),
            pltpu.make_async_copy(w_hbm.at[ocean], w.at[ocean], w_sem.at[i]),
        )

    for i in range(W_CHUNKS):
        for copy in bring(i):
            copy.start()

    barrier = pltpu.get_barrier_semaphore()

    def greet(i, carry):
        d = (me + i) % DEV
        pl.semaphore_signal(barrier, 1, device_id=(d // 2, d % 2), device_id_type=MESH)
        return carry

    lax.fori_loop(1, DEV, greet, 0)

    small[0].wait()
    small[1].wait()
    own = owner[...]
    blk = block[...]
    drow = iota((DEV, OB), 0)
    earlier = (iota((OB, OB), 0) < iota((OB, OB), 1)).astype(BF16)
    hit = [own[k : k + 1, :] == drow for k in range(2)]
    ones = [h.astype(F32) for h in hit]
    rank = [jnp.dot(o.astype(BF16), earlier, preferred_element_type=F32) for o in ones]
    rank[1] = rank[1] + jnp.sum(ones[0], axis=1, keepdims=True)
    wide = blk + (WIDE - ACROSS) * (
        (blk >= ACROSS).astype(jnp.int32)
        + (blk >= 2 * ACROSS).astype(jnp.int32)
        + (blk >= 3 * ACROSS).astype(jnp.int32)
    )
    wide = (wide + 1).astype(F32)
    position = iota((1, OB), 1).astype(F32) * 2.0
    first = iota((8, OB), 0)
    facts = []
    for k in range(2):
        facts.append(
            jnp.where(
                first == 0,
                wide[k : k + 1, :],
                jnp.where(first == 1, position + float(k - 2 * OB), 0.0),
            ).astype(BF16)
        )
    found = []
    for r in range(CAP):
        total = jnp.zeros((8, DEV), F32)
        for k in range(2):
            mine = jnp.where(rank[k] == float(r), ones[k], 0.0).astype(BF16)
            total = total + lax.dot_general(
                facts[k], mine, (((1,), (1,)), ((), ())), preferred_element_type=F32
            )
        found.append(total)
    row8 = iota((8, DEV), 0)
    index = jnp.zeros((8, DEV), F32)
    names = jnp.zeros((8, DEV), F32)
    for r in range(CAP):
        index = jnp.where(row8 == r, found[r][1:2, :] + float(2 * OB), index)
        names = jnp.where(row8 == r, found[r][0:1, :] - 1.0, names)
    index_v[...] = jnp.clip(index.astype(jnp.int32), 0, 2 * OB)
    to_smem = pltpu.make_async_copy(index_v, index_s, idx_sem)
    to_smem.start()
    labels[...] = jnp.concatenate([names, jnp.zeros((DEV - 8, DEV), F32)], axis=0).T

    padded[:, :, 640:VC] = jnp.zeros((3, ROWS, 128), F32)
    small[4].wait()
    small[5].wait()
    padded[0, :, 0:COLS] = east[...]
    row_global = tile * ROWS + iota((ROWS, COLS), 0)
    padded[1, :, 0:COLS] = jnp.where(row_global < 64 * ROWS - 1, north[...], 0.0)
    top = iota((8, VC), 0) == 0

    def lay(r, carry):
        at = pl.ds(pl.multiple_of(r * 8, 8), 8)
        ease, norse = padded[0, at, :], padded[1, at, :]
        for i in range(8):
            coef[HALO + 8 * r + i] = jnp.where(top, ease[i : i + 1, :], norse[i : i + 1, :])
        return carry

    lax.fori_loop(0, ROWS // 8, lay, 0)

    gather_edges(coef, col_out.at[0])

    items[0, 2 * OB] = jnp.zeros((8, BLK), F32)
    items[1, 2 * OB] = jnp.zeros((8, BLK), F32)
    small[2].wait()
    frac = [np.float32(h) / np.float32(HOURS) for h in range(HOURS)]
    blank = jnp.zeros((1, BLK), F32)

    def timed(p):
        at = pl.ds(pl.multiple_of(p * BLK, BLK), BLK)
        early = late = None
        for h in range(HOURS):
            x = flux[h, :, at].astype(F32)
            early = x if h == 0 else early + (np.float32(1.0) - frac[h]) * x
            if h:
                late = frac[h] * x if h == 1 else late + frac[h] * x
        mask = wet[pl.ds(p, 1), :].astype(F32)
        return jnp.concatenate([early * mask, late * mask, blank, blank], axis=0).astype(BF16)

    nothing = jnp.zeros((16, BLK), BF16)

    def chunk(i, carry):
        for copy in bring(i):
            copy.wait()
        for g in range(0, blocks, 2):
            p = i * blocks + g
            left = jnp.concatenate(
                [
                    jnp.concatenate([timed(p), nothing], axis=1),
                    jnp.concatenate([nothing, timed(p + 1)], axis=1),
                ],
                axis=0,
            )
            right = jnp.concatenate(
                [jnp.concatenate([w[p + e, 0], w[p + e, 1]], axis=1) for e in range(2)], axis=0
            )
            made = jnp.dot(left, right, preferred_element_type=F32)
            for e in range(2):
                for k in range(2):
                    for half in range(2):
                        items[half, 2 * (p + e) + k] = made[
                            16 * e + 8 * half : 16 * e + 8 * half + 8, BLK * k : BLK * k + BLK
                        ]
        return carry

    lax.fori_loop(0, W_CHUNKS, chunk, 0)

    to_smem.wait()
    pl.semaphore_wait(barrier, DEV - 1)

    def pack(d, into):
        for r in range(CAP):
            at = index_s[r, d]
            for half, (start, count) in enumerate(PARTS):
                row = r * CH + start
                into[row : row + count, :] = items[half, at][0:count, :]
        into[CAP * CH : CAP * CH + 1, :] = labels[pl.ds(d, 1), :]

    for g in range(GROUPS):

        def send(j, carry, g=g):
            t, u = peer_of(tile, sub, j)
            pack(t * 2 + u, stage.at[j])
            pltpu.make_async_remote_copy(
                src_ref=stage.at[j],
                dst_ref=recv.at[j],
                send_sem=send_sem,
                recv_sem=recv_sem.at[g],
                device_id=(t, u),
                device_id_type=MESH,
            ).start()
            return carry

        lax.fori_loop(max(1, EACH * g), EACH * (g + 1), send, 0)

    coef_copies = halo_start(
        coef, True, tile, sub, col_out.at[0], col_in.at[0], cor_in.at[0], halo_send.at[0], halo_recv.at[0]
    )
    pack(me, recv.at[0])

    small[3].wait()
    padded[2, :, 0:COLS] = land[...].astype(F32)
    slot_rows = iota((4 * WIDE, CAP * EACH), 0).astype(F32)

    def arrive(g):
        low = max(1, EACH * g)
        everything = recv.at[pl.ds(low, EACH * (g + 1) - low)]
        pltpu.make_async_copy(everything, everything, recv_sem.at[g]).wait()
        here = slice(EACH * g, EACH * (g + 1))
        named = recv[here, CAP * CH, :].T
        line = jnp.concatenate([named[r : r + 1, :] for r in range(CAP)], axis=1)
        return (slot_rows == line).astype(BF16)

    def add_group(g, picked, first, last):
        here = slice(EACH * g, EACH * (g + 1))
        for f in range(first, last, 2):
            got = jnp.concatenate(
                [
                    jnp.concatenate(
                        [recv[here, r * CH + f + e, :].astype(BF16) for r in range(CAP)], axis=0
                    )
                    for e in range(2)
                ],
                axis=1,
            )
            both = jnp.dot(picked, got, preferred_element_type=F32)
            for e in range(2):
                part = both[:, 128 * e : 128 * e + 128]
                sums[f + e] = part if g == 0 else sums[f + e] + part

    def assemble(half, grid):
        start, count = PARTS[half]
        none = jnp.zeros((8, 128), F32)

        def place(r, carry):
            for q in range(6):
                lanes = slice(128 * q, 128 * q + 128)
                at = pl.ds(pl.multiple_of(r * WIDE + 8 * q, 8), 8)
                xs = [sums[start + f, at, :] if f < count else none for f in range(8)]
                xs = swap_vregs_lanes(swap_vregs_rows(xs))
                sea = padded[2, pl.ds(pl.multiple_of(r * 8, 8), 8), lanes]
                for i in range(8):
                    grid[HALO + 8 * r + i, :, lanes] = xs[i] * sea[i : i + 1, :]
            return carry

        lax.fori_loop(0, ROWS // 8, place, 0)
        return halo_start(
            grid,
            False,
            tile,
            sub,
            col_out.at[1 + half],
            col_in.at[1 + half],
            cor_in.at[1 + half],
            halo_send.at[1 + half],
            halo_recv.at[1 + half],
        )

    def smooth(half, copies, grid):
        start, count = PARTS[half]
        halo_finish(copies, grid, col_in.at[1 + half], cor_in.at[1 + half])
        def lines(src, dst, base, n):
            v = src[base]
            below = north_b[base - 1] * (v - src[base - 1])
            for k in range(n):
                at = base + k
                above = src[at + 1]
                rise = north_b[at] * (above - v)
                east_side = east_b[at] * (pltpu.roll(v, VC - 1, 1) - v)
                west_side = west_b[at] * (v - pltpu.roll(v, 1, 1))
                dst[at] = v + (east_side - west_side) + (rise - below)
                v, below = above, rise

        for turn in range(PASSES):
            src, dst = (grid, spare) if turn % 2 == 0 else (spare, grid)
            low, count_rows = turn + 1, VR - 2 - 2 * turn

            def block_of(n, carry, src=src, dst=dst, low=low):
                lines(src, dst, low + 8 * n, 8)
                return carry

            lax.fori_loop(0, count_rows // 8, block_of, 0)
            if count_rows % 8:
                lines(src, dst, low + count_rows // 8 * 8, count_rows % 8)

        def turn_back(r, carry):
            for q in range(6):
                lanes = slice(128 * q, min(128 * q + 128, COLS))
                xs = [grid[HALO + 8 * r + i, :, 128 * q : 128 * q + 128] for i in range(8)]
                xs = swap_vregs_rows(xs)
                for c in range(count):
                    out[start + c, pl.ds(pl.multiple_of(r * 8, 8), 8), lanes] = xs[c][
                        :, 0 : min(128, COLS - 128 * q)
                    ]
            return carry

        lax.fori_loop(0, ROWS // 8, turn_back, 0)

    for g in range(GROUPS // 2):
        add_group(g, arrive(g), 0, CH)
    for g in range(GROUPS // 2, GROUPS - 1):
        add_group(g, arrive(g), 0, CH)
    final = arrive(GROUPS - 1)
    halves = []
    for half, grid in ((0, grid_a), (1, grid_b)):
        start, count = PARTS[half]
        add_group(GROUPS - 1, final, start, start + count)
        halves.append(assemble(half, grid))
    halo_finish(coef_copies, coef, col_in.at[0], cor_in.at[0])

    def spread(i, carry):
        both = coef[i]
        ease = jnp.broadcast_to(both[0:1, :], (8, VC))
        east_b[i] = ease
        west_b[i] = pltpu.roll(ease, 1, 1)
        north_b[i] = jnp.broadcast_to(both[1:2, :], (8, VC))
        return carry

    lax.fori_loop(0, VR, spread, 0)

    smooth(0, halves[0], grid_a)
    smooth(1, halves[1], grid_b)

    everything = stage.at[pl.ds(1, DEV - 1)]
    pltpu.make_async_copy(everything, everything, send_sem).wait()


def on_device(
    adjoint_flux,
    ocean_wet,
    intersection_weight,
    pair_owner,
    pair_block,
    land_sea,
    east_coef,
    north_coef,
):
    vmem = pltpu.VMEM
    dma = pltpu.SemaphoreType.DMA
    return pl.pallas_call(
        kernel,
        out_shape=pltpu.VMEM((2 * FIELDS, ROWS, COLS), F32),
        in_specs=[pl.BlockSpec(memory_space=pl.ANY)] * 8,
        out_specs=pl.BlockSpec(memory_space=pltpu.VMEM),
        scratch_shapes=[
            vmem((HOURS, FIELDS, OB * BLK), BF16),
            vmem((OB, BLK), jnp.int32),
            vmem((OB, 2, BLK, BLK), BF16),
            vmem((2, OB), jnp.int32),
            vmem((2, OB), jnp.int32),
            vmem((ROWS, COLS), jnp.int32),
            vmem((ROWS, COLS), F32),
            vmem((ROWS, COLS), F32),
            vmem((2, 2 * OB + 1, 8, BLK), F32),
            vmem((8, DEV), jnp.int32),
            pltpu.SMEM((8, DEV), jnp.int32),
            vmem((DEV, DEV), F32),
            vmem((DEV, CAP * CH + 1, BLK), F32),
            vmem((DEV, CAP * CH + 1, BLK), F32),
            vmem((CH, 4 * WIDE, 128), F32),
            vmem((3, ROWS, VC), F32),
            vmem((VR, 8, VC), F32),
            vmem((VR, 8, VC), F32),
            vmem((VR, 8, VC), F32),
            vmem((VR, 8, VC), F32),
            vmem((VR, 8, VC), F32),
            vmem((VR, 8, VC), F32),
            vmem((VR, 8, VC), F32),
            vmem((3, 2, 8, 128), F32),
            vmem((3, 2, 8, 128), F32),
            vmem((3, 2, 8, 128), F32),
            dma((6,)),
            dma((W_CHUNKS,)),
            dma((F_CHUNKS,)),
            dma,
            dma,
            dma((GROUPS,)),
            dma((3, 5)),
            dma((3, 5)),
        ],
        compiler_params=pltpu.CompilerParams(
            collective_id=0, has_side_effects=True, vmem_limit_bytes=54 * 2**20
        ),
        cost_estimate=pl.CostEstimate(
            flops=4 * 10**8, bytes_accessed=12 * 10**6, transcendentals=0
        ),
    )(
        adjoint_flux,
        ocean_wet.reshape(OB, BLK),
        intersection_weight,
        pair_owner.T,
        pair_block.T,
        land_sea,
        east_coef,
        north_coef,
    )


def solution(mesh):
    in_specs = (
        P(None, None, ("tile", "sub")),
        P(("tile", "sub")),
        P(("tile", "sub"), None, None, None),
        P(("tile", "sub"), None),
        P(("tile", "sub"), None),
        P("tile", "sub"),
        P("tile", "sub"),
        P("tile", "sub"),
    )
    out_specs = P(None, "tile", "sub")
    return jax.shard_map(
        on_device, mesh=mesh, in_specs=in_specs, out_specs=out_specs, check_vma=False
    )
```
